32 devices in a mesh: dy: 8 (over y, x, core), dx: 4 (over z).
Axes of the slice: x: 2, y: 2, z: 4, core: 2. Of those that a mesh axis runs over, the one named last changes fastest.
Arguments:
- heights: float32 [4096, 2048], P('dy', 'dx'), may hold values from -4 to 4
- albedo: float32 [4096, 2048], P('dy', 'dx'), may hold values from 0.5 to 1.5
- observed: bfloat16 [512, 384, 384], P(('dy', 'dx')), may hold values from -2 to 2
- resample: bfloat16 [512, 2, 384, 384], P(('dy', 'dx')), may hold values from -1 to 1
- exposure: float32 [4, 16], P('dx'), may hold values from -0.5 to 0.5
- sun_azimuth: float32 [4, 16], P('dx'), may hold values from -3.140625 to 3.140625
- sun_elevation: float32 [4, 16], P('dx'), may hold values from 0.02 to 0.3
- send_plan: int32 [8, 4, 4, 24], P('dy', 'dx'), may hold values from 0 to 128, as said below
- recv_plan: int32 [8, 4, 16], P('dy', 'dx'), may hold values from 0 to 23, as said below
Outputs:
- height_gradient: float32 [4096, 2048], P('dy', 'dx')
- camera_gradient: float32 [4, 16, 7], P('dx', 'dy')
The draws below stay inside these ranges and needn't reach their ends.
Inputs may be any that keep to these rules, and one draw needn't show every extreme that they name: send_plan[s, c, :, r * 3 + j] describes slot j of the crops that the DEM tile (s, c) serves to the device (r, c): row offset and column offset of the crop's window in the tile (multiples of 128, at most 128 and 128), the image m, and 1; unused slots are all zeros. Every device is served exactly 3 crops by at least one tile. recv_plan[r, c, m] = s * 3 + j names the used slot send_plan[s, c, :, r * 3 + j] whose image is m; the values of one device are distinct.
All inputs are finite; a program needn't handle non-finite values.
Results may differ from the reference program's by a relative error of at most 0.005.
Values may be sent and summed in bfloat16 or wider, within the bound.
A program may use at most 384 MiB of HBM per device.

```python
import jax
import jax.numpy as jnp
from jax import lax

TY = 512
TX = 512
IMG_BAND = 16
CROP = 384
BLK = 128
MOST = 3
NY = 4096
NX = 2048
CROPS = 512
N_DY = 8
N_DX = 4


DENSE_WEIGHT = 0.4


DENSE_LIMIT = 0.25


def plan_tables(key):
    base_key = jax.random.fold_in(key, 4242)
    key_rank, key_full, key_row, key_col = jax.random.split(base_key, 4)
    slot_count = N_DY * MOST
    owners = N_DY * N_DX
    slot_rank = jax.vmap(lambda rank_key: jax.random.permutation(rank_key, slot_count))(jax.random.split(key_rank, owners))
    slot_rank = slot_rank.reshape(N_DY, N_DX, slot_count).astype(jnp.int32)
    full_source = jax.random.randint(key_full, (N_DY, N_DX), 0, N_DY).astype(jnp.int32)
    full_source = full_source.at[0, 0].set(N_DY - 1)
    slot_source = jnp.arange(slot_count, dtype=jnp.int32) // MOST
    scores = jnp.where(slot_source[None, None, :] == full_source[:, :, None], -1, slot_rank)
    slot_order = jnp.argsort(scores, axis=-1, stable=True)
    chosen = slot_order[:, :, :IMG_BAND].astype(jnp.int32)
    row_steps = TY // BLK - CROP // BLK + 1
    col_steps = TX // BLK - CROP // BLK + 1
    shape_all = (N_DY, N_DX, IMG_BAND)
    row_off = jax.random.randint(key_row, shape_all, 0, row_steps).astype(jnp.int32) * BLK
    col_off = jax.random.randint(key_col, shape_all, 0, col_steps).astype(jnp.int32) * BLK
    image_ids = jnp.broadcast_to(jnp.arange(IMG_BAND, dtype=jnp.int32)[None, None, :], shape_all)
    row_off = jnp.where(image_ids == 0, TY - CROP, row_off)
    col_off = jnp.where(image_ids == 0, TX - CROP, col_off)
    dest_row = jnp.broadcast_to(jnp.arange(N_DY, dtype=jnp.int32)[:, None, None], shape_all)
    column = jnp.broadcast_to(jnp.arange(N_DX, dtype=jnp.int32)[None, :, None], shape_all)
    source = chosen // MOST
    lane_index = dest_row * MOST + chosen % MOST
    plan_table = jnp.zeros((N_DY, N_DX, 4, slot_count), jnp.int32)
    plan_table = plan_table.at[source, column, 0, lane_index].set(row_off)
    plan_table = plan_table.at[source, column, 1, lane_index].set(col_off)
    plan_table = plan_table.at[source, column, 2, lane_index].set(image_ids)
    plan_table = plan_table.at[source, column, 3, lane_index].set(jnp.ones(shape_all, jnp.int32))
    return (plan_table, chosen)


def draw_send_plan(key, part):
    return plan_tables(key)[0]


def draw_recv_plan(key, part):
    return plan_tables(key)[1]


def one_matrix_pair(crop_key):
    key_frac, key_shift, key_dense = jax.random.split(crop_key, 3)
    frac = jax.random.uniform(key_frac, (2, CROP, 1), jnp.float32, 0.0, 1.0)
    offset = jax.random.randint(key_shift, (2, 1, 1), -3, 4).astype(jnp.int32)
    row_pos = jnp.arange(CROP, dtype=jnp.int32)[:, None]
    col_pos = jnp.arange(CROP, dtype=jnp.int32)[None, :]
    distance = (col_pos - row_pos)[None] - offset
    frac_sq = frac * frac
    frac_cu = frac_sq * frac
    tap_minus = 0.5 * (-frac_cu + 2.0 * frac_sq - frac)
    tap_zero = 0.5 * (3.0 * frac_cu - 5.0 * frac_sq + 2.0)
    tap_one = 0.5 * (-3.0 * frac_cu + 4.0 * frac_sq + frac)
    tap_two = 0.5 * (frac_cu - frac_sq)
    band = jnp.where(distance == -1, tap_minus, 0.0) + jnp.where(distance == 0, tap_zero, 0.0) + jnp.where(distance == 1, tap_one, 0.0) + jnp.where(distance == 2, tap_two, 0.0)
    spread = DENSE_WEIGHT / CROP ** 0.5
    dense = jax.random.normal(key_dense, (2, CROP, CROP), jnp.float32) * spread
    band_scale = 0.75
    dense = jnp.clip(dense, -DENSE_LIMIT, DENSE_LIMIT)
    return (band_scale * band + dense).astype(jnp.bfloat16)


def draw_resample(key, part):
    crop_keys = jax.random.split(jax.random.fold_in(key, 99), CROPS)
    return lax.map(one_matrix_pair, crop_keys)


def levels(own_key, dims, shards, low, high):
    def one(axis_at, parts):
        draws = jax.random.uniform(jax.random.fold_in(jax.random.fold_in(own_key, 6), axis_at), (parts,), jnp.float32, low / len(shards), high / len(shards))
        return jnp.repeat(jnp.exp(draws), dims[axis_at] // parts).reshape((-1,) + (1,) * (len(dims) - axis_at - 1))

    level = one(*shards[0])
    for cut in shards[1:]:
        level = level * one(*cut)
    return level


def centred(stream_key, dims, width, reach, pieces=(), kind=jnp.bfloat16):
    values = jax.random.normal(stream_key, dims, jnp.float32) * width
    if len(pieces) > 0:
        values = levels(stream_key, dims, pieces, -0.22, 0.18) * values
    return jnp.clip(values, min=-reach, max=reach).astype(kind)


def setup_inputs(seed: int = 0) -> dict:
    keys = jax.random.split(jax.random.key(seed), 10)
    return {
        "heights": centred(keys[0], (NY, NX), 0.5, 4.0, ((0, 8), (1, 4)), jnp.float32),
        "albedo": jnp.clip(0.5 + 1.0 * jax.random.uniform(keys[1], (NY, NX), jnp.float32) ** levels(keys[1], (NY, NX), ((0, 8), (1, 4)), -0.2, 0.2), 0.5, 1.5),
        "observed": centred(keys[2], (CROPS, CROP, CROP), 0.3, 2.0, ((0, 32),)),
        "resample": draw_resample(jax.random.fold_in(keys[9], 71), 0),
        "exposure": jnp.clip(jax.random.uniform(keys[4], (N_DX, IMG_BAND), jnp.float32, -0.5, 0.5) * levels(keys[4], (N_DX, IMG_BAND), ((0, 4),), -0.4, 0.0), -0.5, 0.5),
        "sun_azimuth": jnp.clip(jax.random.uniform(keys[5], (N_DX, IMG_BAND), jnp.float32, -3.140625, 3.140625), -3.140625, 3.140625),
        "sun_elevation": jnp.clip(0.02 + 0.28 * jax.random.uniform(keys[6], (N_DX, IMG_BAND), jnp.float32) ** levels(keys[6], (N_DX, IMG_BAND), ((0, 4),), -0.2, 0.2), 0.02, 0.3),
        "send_plan": draw_send_plan(jax.random.fold_in(keys[9], 71), 0),
        "recv_plan": draw_recv_plan(jax.random.fold_in(keys[9], 71), 0),
    }


SMOOTHING_WEIGHT = 0.02

def slopes(padded):
    slope_x = (padded[1:-1, 2:] - padded[1:-1, :-2]) * 0.5
    slope_y = (padded[2:, 1:-1] - padded[:-2, 1:-1]) * 0.5
    return (slope_x, slope_y)

def laplace(padded):
    return padded[:-2, 1:-1] + padded[2:, 1:-1] + padded[1:-1, :-2] + padded[1:-1, 2:] - 4.0 * padded[1:-1, 1:-1]

def shading(slope_x, slope_y, albedo):
    length = jnp.sqrt(1.0 + slope_x * slope_x + slope_y * slope_y)
    normal = jnp.stack([-slope_x, -slope_y, jnp.ones_like(slope_x)])
    return albedo[None] * normal / length[None]

def sun_vectors(solar_azimuth, elevation):
    return jnp.stack([jnp.cos(elevation) * jnp.cos(solar_azimuth), jnp.cos(elevation) * jnp.sin(solar_azimuth), jnp.sin(elevation)])

def edge_diff(values):
    step_diff = values[..., 1:] - values[..., :-1]
    return jnp.concatenate([step_diff[..., :1], 0.5 * (step_diff[..., 1:] + step_diff[..., :-1]), step_diff[..., -1:]], axis=-1)

def crop_terms(predicted, residual):
    crop_size = predicted.shape[-1]
    coordinate = (jnp.arange(crop_size, dtype=jnp.float32) - 0.5 * (crop_size - 1)) / crop_size
    deriv_u = edge_diff(predicted)
    deriv_v = jnp.swapaxes(edge_diff(jnp.swapaxes(predicted, -1, -2)), -1, -2)
    resid_u = residual * deriv_u
    resid_v = residual * deriv_v
    col_coord = coordinate[None, None, :]
    row_coord = coordinate[None, :, None]
    sum_list = [lax.optimization_barrier(jnp.sum(resid_u, axis=(1, 2))), lax.optimization_barrier(jnp.sum(resid_u * col_coord, axis=(1, 2))), lax.optimization_barrier(jnp.sum(resid_u * row_coord, axis=(1, 2))), lax.optimization_barrier(jnp.sum(resid_v, axis=(1, 2))), lax.optimization_barrier(jnp.sum(resid_v * col_coord, axis=(1, 2))), lax.optimization_barrier(jnp.sum(resid_v * row_coord, axis=(1, 2)))]
    pose_part = jnp.stack(sum_list, axis=-1) / crop_size
    exposure_part = lax.optimization_barrier(jnp.sum(residual * predicted, axis=(1, 2))) / (crop_size * crop_size)
    return jnp.concatenate([pose_part, exposure_part[:, None]], axis=-1)

def render(shaded, observed, resample, exposure_gain):
    row_mat = resample[:, 0].astype(jnp.float32)
    col_mat = resample[:, 1].astype(jnp.float32)
    first_pass = jnp.einsum('nij,njk->nik', row_mat, shaded.astype(jnp.float32)).astype(jnp.bfloat16)
    predicted = exposure_gain[:, None, None] * jnp.einsum('nil,nkl->nik', first_pass.astype(jnp.float32), col_mat)
    residual = predicted - observed.astype(jnp.float32)
    crop_sums = crop_terms(predicted, residual)
    weighted = (exposure_gain[:, None, None] * residual).astype(jnp.bfloat16)
    back_pass = jnp.einsum('nji,njk->nik', row_mat, weighted.astype(jnp.float32)).astype(jnp.bfloat16)
    crop_grad = jnp.einsum('njk,nkl->njl', back_pass.astype(jnp.float32), col_mat).astype(jnp.bfloat16)
    return (crop_sums, crop_grad)

def reference(heights, albedo, observed, resample, exposure, sun_azimuth, sun_elevation, send_plan, recv_plan):
    padded = jnp.pad(heights, 1)
    slope_x, slope_y = slopes(padded)
    fields = shading(slope_x, slope_y, albedo)
    sun_table = sun_vectors(sun_azimuth, sun_elevation)
    crop_ids = jnp.arange(N_DY * N_DX * IMG_BAND, dtype=jnp.int32)
    dest_row = crop_ids // (N_DX * IMG_BAND)
    column = crop_ids // IMG_BAND % N_DX
    image_ids = crop_ids % IMG_BAND
    slot_ids = recv_plan.reshape(-1).astype(jnp.int32)
    source = slot_ids // MOST
    lane_index = dest_row * MOST + slot_ids % MOST
    top_row = (source * TY + send_plan[source, column, 0, lane_index]).astype(jnp.int32)
    left_col = (column * TX + send_plan[source, column, 1, lane_index]).astype(jnp.int32)
    crop_sun = sun_table[:, column, image_ids]
    exposure_gain = jnp.exp(exposure[column, image_ids])

    def cut(crop_index):
        image_window = lax.dynamic_slice(fields, (jnp.int32(0), top_row[crop_index], left_col[crop_index]), (3, CROP, CROP))
        return lax.optimization_barrier(jnp.sum(crop_sun[:, crop_index][:, None, None] * image_window, axis=0)).astype(jnp.bfloat16)
    shaded = lax.map(cut, crop_ids)
    groups = N_DY * N_DX

    def group_render(bundle_in):
        return render(bundle_in[0], bundle_in[1], bundle_in[2], bundle_in[3])
    crop_sums, crop_grad = lax.map(group_render, (shaded.reshape(groups, IMG_BAND, CROP, CROP), observed.reshape(groups, IMG_BAND, CROP, CROP), resample.reshape(groups, IMG_BAND, 2, CROP, CROP), exposure_gain.reshape(groups, IMG_BAND)))
    crop_grad = crop_grad.reshape(-1, CROP, CROP)

    def place(running, crop_index):
        start = (jnp.int32(0), top_row[crop_index], left_col[crop_index])
        image_window = lax.dynamic_slice(running, start, (3, CROP, CROP))
        update = image_window + crop_sun[:, crop_index][:, None, None] * crop_grad[crop_index].astype(jnp.float32)[None]
        return (lax.dynamic_update_slice(running, update, start), None)
    field_grads, _ = lax.scan(place, jnp.zeros((3, NY, NX), jnp.float32), crop_ids)

    def shade_local(slope_a, slope_b):
        return shading(slope_a, slope_b, albedo)
    _, pull_back = jax.vjp(shade_local, slope_x, slope_y)
    grad_x, grad_y = pull_back(field_grads)
    padded_x = jnp.pad(grad_x, 1)
    padded_y = jnp.pad(grad_y, 1)
    data_term_gradient = (padded_x[1:-1, :-2] - padded_x[1:-1, 2:]) * 0.5 + (padded_y[:-2, 1:-1] - padded_y[2:, 1:-1]) * 0.5
    laplacian = laplace(padded)
    smoothness_term = laplace(jnp.pad(laplacian, 1))
    height_gradient = data_term_gradient + SMOOTHING_WEIGHT * smoothness_term
    camera_gradient = lax.optimization_barrier(jnp.sum(crop_sums.reshape(N_DY, N_DX, IMG_BAND, 7), axis=0))
    return (height_gradient, camera_gradient)
```

```python
import functools

import jax
import jax.numpy as jnp
from jax import lax
from jax.experimental import pallas as pl
from jax.experimental.pallas import tpu as pltpu
from jax.sharding import PartitionSpec as P

SMOOTHING_WEIGHT = 0.02
MESH = pl.DeviceIdType.MESH
VMEM_BYTES = 56 * 1024 * 1024


def shifted(block, axis, dim, width):
    count = lax.axis_size(axis)
    forward = [(i, i + 1) for i in range(count - 1)]
    backward = [(target, source) for source, target in forward]
    low = lax.ppermute(
        lax.slice_in_dim(block, block.shape[dim] - width, None, axis=dim), axis, forward
    )
    high = lax.ppermute(lax.slice_in_dim(block, 0, width, axis=dim), axis, backward)
    return low, high


def padded_2(block, sides, width):
    for axis, dim in sides:
        low, high = shifted(block, axis, dim, width)
        block = jnp.concatenate([low, block, high], axis=dim)
    return block


def slopes(padded):
    slope_x = (padded[1:-1, 2:] - padded[1:-1, :-2]) * 0.5
    slope_y = (padded[2:, 1:-1] - padded[:-2, 1:-1]) * 0.5
    return (slope_x, slope_y)


def laplace(padded):
    return (
        padded[:-2, 1:-1]
        + padded[2:, 1:-1]
        + padded[1:-1, :-2]
        + padded[1:-1, 2:]
        - 4.0 * padded[1:-1, 1:-1]
    )


def shading(slope_x, slope_y, albedo):
    up = albedo * lax.rsqrt(1.0 + slope_x * slope_x + slope_y * slope_y)
    return jnp.stack([-slope_x * up, -slope_y * up, up])


def sun_vectors(solar_azimuth, elevation):
    return jnp.stack(
        [
            jnp.cos(elevation) * jnp.cos(solar_azimuth),
            jnp.cos(elevation) * jnp.sin(solar_azimuth),
            jnp.sin(elevation),
        ]
    )


def bit_count(count):
    bits = count.bit_length() - 1
    assert 1 << bits == count
    return bits


def flipped(index, mask, bits):
    for bit in range(bits):
        if mask >> bit & 1:
            weight = 1 << bit
            index = index + weight * (1 - 2 * ((index // weight) % 2))
    return index


def bit_orders(bits):
    up = list(range(1, bits))
    return (up, up[::-1])


def all_masks(order):
    masks = [0]
    for bit in order:
        masks = masks + [mask | 1 << bit for mask in masks]
    return masks


def gather_kernel(n, copies, own_ref, plan_ref, out_ref, plans_ref, send, recv, psend, precv, lsem):
    bits = bit_count(n)
    me = lax.axis_index("dy")
    half = own_ref.shape[1] // 2
    barrier = pltpu.get_barrier_semaphore()
    for step in range(1, n):
        pl.semaphore_signal(
            barrier, inc=1, device_id={"dy": lax.rem(me + step, n)}, device_id_type=MESH
        )
    pl.semaphore_wait(barrier, n - 1)

    number = iter(range(copies))

    def rows(part):
        return pl.ds(part * half, half)

    def make(mask, part, bit):
        tile = flipped(me, mask, bits)
        source = own_ref if mask == 0 else out_ref.at[tile]
        c = next(number)
        return pltpu.make_async_remote_copy(
            src_ref=source.at[:, rows(part), :],
            dst_ref=out_ref.at[tile, :, rows(part), :],
            send_sem=send.at[c],
            recv_sem=recv.at[c],
            device_id={"dy": flipped(me, 1 << bit, bits)},
            device_id_type=MESH,
        )

    orders = bit_orders(bits)
    started = []
    arriving = {}

    def forward(mask, part, over):
        copy = make(mask, part, over)
        copy.start()
        started.append(copy)
        arriving[(mask | 1 << over, part)] = copy

    def later(mask, order):
        seen = [k for k, bit in enumerate(order) if mask >> bit & 1]
        return order[(max(seen) + 1 if seen else 0) :]

    for position in range(bits - 1):
        for part, order in enumerate(orders):
            forward(0, part, order[position])
    plan_copies = []
    for step in range(1, n):
        to = lax.rem(me + step, n)
        copy = pltpu.make_async_remote_copy(
            src_ref=plan_ref.at[to],
            dst_ref=plans_ref.at[me],
            send_sem=psend.at[step - 1],
            recv_sem=precv.at[step - 1],
            device_id={"dy": to},
            device_id_type=MESH,
        )
        copy.start()
        plan_copies.append(copy)
    for part in range(2):
        forward(0, part, 0)
    local = pltpu.make_async_copy(own_ref, out_ref.at[me], lsem.at[0])
    local.start()
    local_plan = pltpu.make_async_copy(plan_ref.at[me], plans_ref.at[me], lsem.at[1])
    local_plan.start()
    mask_lists = [all_masks(order)[1:] for order in orders]
    for position in range(len(mask_lists[0])):
        for part, order in enumerate(orders):
            mask = mask_lists[part][position]
            arriving[(mask, part)].wait_recv()
            for bit in later(mask, order):
                forward(mask, part, bit)
            forward(mask, part, 0)
    for (mask, part), copy in arriving.items():
        if mask & 1:
            copy.wait_recv()
    for copy in started:
        copy.wait_send()
    for copy in plan_copies:
        copy.wait()
    local.wait()
    local_plan.wait()


def gather_tiles(own, plan_by_dest, n):
    bits = bit_count(n)
    high = n // 2
    copies = 2 * (high - 1) + 2 * high
    return pl.pallas_call(
        functools.partial(gather_kernel, n, copies),
        out_shape=(
            jax.ShapeDtypeStruct((n,) + own.shape, own.dtype),
            jax.ShapeDtypeStruct(plan_by_dest.shape, plan_by_dest.dtype),
        ),
        in_specs=[pl.BlockSpec(memory_space=pl.ANY)] * 2,
        out_specs=(pl.BlockSpec(memory_space=pl.ANY),) * 2,
        scratch_shapes=[
            pltpu.SemaphoreType.DMA((copies,)),
            pltpu.SemaphoreType.DMA((copies,)),
            pltpu.SemaphoreType.DMA((n - 1,)),
            pltpu.SemaphoreType.DMA((n - 1,)),
            pltpu.SemaphoreType.DMA((2,)),
        ],
        compiler_params=pltpu.CompilerParams(collective_id=0, has_side_effects=True),
        name="gather_tiles",
    )(own, plan_by_dest)


def render_kernel(
    plans, pick, used, light, tiles_ref, mats_ref, seen_ref, grads_ref, sums_ref, total
):
    tile, slot = pl.program_id(0), pl.program_id(1)
    most = pl.num_programs(1)
    step = tile * most + slot
    size = seen_ref.shape[-1]

    @pl.when(slot == 0)
    def _():
        total[...] = jnp.zeros_like(total)

    @pl.when(used[step] == 1)
    def _():
        image = pick[step]
        rows = pl.ds(pl.multiple_of(plans[tile, 0, slot], 128), size)
        cols = pl.ds(pl.multiple_of(plans[tile, 1, slot], 128), size)
        sun_x, sun_y, sun_z = light[0, image], light[1, image], light[2, image]
        gain = light[3, image]

        def field(k):
            return tiles_ref[0, k, rows, cols].astype(jnp.float32)

        shaded = (sun_x * field(0) + sun_y * field(1) + sun_z * field(2)).astype(jnp.bfloat16)
        first = jnp.dot(mats_ref[0, 0], shaded, preferred_element_type=jnp.float32)
        predicted = gain * lax.dot_general(
            first.astype(jnp.bfloat16),
            mats_ref[0, 1],
            (((1,), (1,)), ((), ())),
            preferred_element_type=jnp.float32,
        )
        residual = predicted - seen_ref[0].astype(jnp.float32)
        weighted = (gain * residual).astype(jnp.bfloat16)
        back = lax.dot_general(
            mats_ref[0, 0], weighted, (((0,), (0,)), ((), ())), preferred_element_type=jnp.float32
        ).astype(jnp.bfloat16)
        crop_grad = jnp.dot(back, mats_ref[0, 1], preferred_element_type=jnp.float32)

        col = lax.broadcasted_iota(jnp.int32, (1, size), 1)
        row = lax.broadcasted_iota(jnp.int32, (size, 1), 0)
        last = size - 1
        right = jnp.where(col == last, predicted, pltpu.roll(predicted, last, 1))
        left = jnp.where(col == 0, predicted, pltpu.roll(predicted, 1, 1))
        below = jnp.where(row == last, predicted, pltpu.roll(predicted, last, 0))
        above = jnp.where(row == 0, predicted, pltpu.roll(predicted, 1, 0))
        col_weight = jnp.where((col == 0) | (col == last), 1.0, 0.5)
        row_weight = jnp.where((row == 0) | (row == last), 1.0, 0.5)
        row_place = (row.astype(jnp.float32) - 0.5 * (size - 1)) / size
        by_u = residual * (right - left)
        by_v = residual * ((below - above) * row_weight)
        sums_ref[image, 0:1] = col_weight * jnp.sum(by_u, axis=0, keepdims=True)
        sums_ref[image, 1:2] = col_weight * jnp.sum(by_u * row_place, axis=0, keepdims=True)
        sums_ref[image, 2:3] = jnp.sum(by_v, axis=0, keepdims=True)
        sums_ref[image, 3:4] = jnp.sum(by_v * row_place, axis=0, keepdims=True)
        sums_ref[image, 4:5] = jnp.sum(residual * predicted, axis=0, keepdims=True)
        sums_ref[image, 5:8] = jnp.zeros((3, size), jnp.float32)

        fx, fy, fz = field(0), field(1), field(2)
        along = (sun_x * fx + sun_y * fy + sun_z * fz) / (fx * fx + fy * fy + fz * fz)
        scaled = crop_grad * fz
        total[0, rows, cols] += scaled * (fx * along - sun_x)
        total[1, rows, cols] += scaled * (fy * along - sun_y)

    @pl.when(slot == most - 1)
    def _():
        grads_ref[0] = total[...].astype(grads_ref.dtype)


def render(plans, pick, used, light, tiles, resample, observed, most):
    n, _, tile_rows, tile_cols = tiles.shape
    crops, size, _ = observed.shape

    def crop_at(t, j, plans, pick, used):
        return pick[t * most + j]

    def inner(plans, pick, used, light, *refs):
        render_kernel(plans, pick, used, light, *refs)

    return pl.pallas_call(
        inner,
        out_shape=(
            jax.ShapeDtypeStruct((n, 2, tile_rows, tile_cols), jnp.bfloat16),
            jax.ShapeDtypeStruct((crops, 8, size), jnp.float32),
        ),
        grid_spec=pltpu.PrefetchScalarGridSpec(
            num_scalar_prefetch=3,
            grid=(n, most),
            in_specs=[
                pl.BlockSpec(memory_space=pltpu.SMEM),
                pl.BlockSpec((1, 3, tile_rows, tile_cols), lambda t, j, *s: (t, 0, 0, 0)),
                pl.BlockSpec((1, 2, size, size), lambda t, j, *s: (crop_at(t, j, *s), 0, 0, 0)),
                pl.BlockSpec((1, size, size), lambda t, j, *s: (crop_at(t, j, *s), 0, 0)),
            ],
            out_specs=(
                pl.BlockSpec((1, 2, tile_rows, tile_cols), lambda t, j, *s: (t, 0, 0, 0)),
                pl.BlockSpec((crops, 8, size), lambda t, j, *s: (0, 0, 0)),
            ),
            scratch_shapes=[pltpu.VMEM((2, tile_rows, tile_cols), jnp.float32)],
        ),
        compiler_params=pltpu.CompilerParams(
            dimension_semantics=("arbitrary", "arbitrary"), vmem_limit_bytes=VMEM_BYTES
        ),
        name="render",
    )(plans, pick, used, light, tiles, resample, observed)


def scatter_kernel(
    n, grads_ref, sums_ref, out_ref, camera_ref, first, later, csums, send, recv, csend, crecv
):
    bits = bit_count(n)
    me = lax.axis_index("dy")
    half = out_ref.shape[1] // 2
    barrier = pltpu.get_barrier_semaphore()
    for step in range(1, n):
        pl.semaphore_signal(
            barrier, inc=1, device_id={"dy": lax.rem(me + step, n)}, device_id_type=MESH
        )
    pl.semaphore_wait(barrier, n - 1)

    number = iter(range(send.shape[0]))
    started = []

    def push(source, target, bit):
        c = next(number)
        copy = pltpu.make_async_remote_copy(
            src_ref=source,
            dst_ref=target,
            send_sem=send.at[c],
            recv_sem=recv.at[c],
            device_id={"dy": flipped(me, 1 << bit, bits)},
            device_id_type=MESH,
        )
        copy.start()
        started.append(copy)
        return copy

    masks = [m << 1 for m in range(n // 2)][::-1]
    pair = {}
    for mask in masks:
        pair[mask] = push(grads_ref.at[flipped(me, mask + 1, bits)], first.at[mask >> 1], 0)
    camera_copies = []
    for step in range(1, n):
        to = lax.rem(me + step, n)
        copy = pltpu.make_async_remote_copy(
            src_ref=sums_ref.at[to],
            dst_ref=csums.at[step - 1],
            send_sem=csend.at[step - 1],
            recv_sem=crecv.at[step - 1],
            device_id={"dy": to},
            device_id_type=MESH,
        )
        copy.start()
        camera_copies.append(copy)

    orders = bit_orders(bits)
    places = iter(range(later.shape[0]))
    coming = {}

    def rows(part):
        return pl.ds(part * half, half)

    for mask in masks:
        pair[mask].wait_recv()
        mine = grads_ref[flipped(me, mask, bits)].astype(jnp.float32)
        both = mine + first[mask >> 1].astype(jnp.float32)
        if mask == 0:
            out_ref[...] = both
        else:
            first[mask >> 1] = both.astype(first.dtype)
            for part, order in enumerate(orders):
                if mask >> order[0] & 1:
                    at = next(places)
                    source = first.at[mask >> 1, :, rows(part), :]
                    copy = push(source, later.at[at], order[0])
                    coming[(part, mask ^ 1 << order[0])] = (copy, at)
    for stage in range(bits - 1):
        for part, order in enumerate(orders):
            landed = [(m, coming.pop((p, m))) for p, m in list(coming) if p == part]
            for mask, (copy, at) in landed:
                copy.wait_recv()
                add = later[at].astype(jnp.float32)
                if mask == 0:
                    out_ref[:, rows(part), :] += add
                else:
                    held = first[mask >> 1, :, rows(part), :].astype(jnp.float32)
                    first[mask >> 1, :, rows(part), :] = (held + add).astype(first.dtype)
                    bit = order[stage + 1]
                    if mask >> bit & 1:
                        to = next(places)
                        source = first.at[mask >> 1, :, rows(part), :]
                        sent = push(source, later.at[to], bit)
                        coming[(part, mask ^ 1 << bit)] = (sent, to)
    camera = sums_ref[me]
    for step in range(1, n):
        camera_copies[step - 1].wait()
        camera = camera + csums[step - 1]
    camera_ref[...] = camera
    for copy in started:
        copy.wait_send()


def scatter_sums(grads, sums, n):
    _, parts, tile_rows, tile_cols = grads.shape
    high = n // 2
    halves = 2 * (high - 1)
    copies = high + halves
    return pl.pallas_call(
        functools.partial(scatter_kernel, n),
        out_shape=(
            jax.ShapeDtypeStruct(grads.shape[1:], jnp.float32),
            jax.ShapeDtypeStruct(sums.shape[1:], jnp.float32),
        ),
        in_specs=[pl.BlockSpec(memory_space=pltpu.VMEM)] * 2,
        out_specs=(pl.BlockSpec(memory_space=pltpu.VMEM),) * 2,
        scratch_shapes=[
            pltpu.VMEM((high, parts, tile_rows, tile_cols), grads.dtype),
            pltpu.VMEM((halves, parts, tile_rows // 2, tile_cols), grads.dtype),
            pltpu.VMEM((n - 1,) + sums.shape[1:], jnp.float32),
            pltpu.SemaphoreType.DMA((copies,)),
            pltpu.SemaphoreType.DMA((copies,)),
            pltpu.SemaphoreType.DMA((n - 1,)),
            pltpu.SemaphoreType.DMA((n - 1,)),
        ],
        compiler_params=pltpu.CompilerParams(
            collective_id=1, has_side_effects=True, vmem_limit_bytes=VMEM_BYTES
        ),
        name="scatter_sums",
    )(grads, sums)


def per_device(
    heights, albedo, observed, resample, exposure, sun_azimuth, sun_elevation, send_plan, recv_plan
):
    n = lax.axis_size("dy")
    tile_rows, tile_cols = heights.shape
    crops, size = observed.shape[0], observed.shape[-1]
    slot_count = send_plan.shape[-1]
    most = slot_count // n
    receive = recv_plan[0, 0]
    sun_table = sun_vectors(sun_azimuth[0], sun_elevation[0])
    light = jnp.concatenate([sun_table, jnp.exp(exposure)])
    slot_ids = jnp.arange(slot_count, dtype=jnp.int32)
    reached = jnp.where(receive[None, :] <= slot_ids[:, None], receive[None, :], -1)
    pick = jnp.argmax(reached, axis=1).astype(jnp.int32)
    used = (jnp.max(reached, axis=1) == slot_ids).astype(jnp.int32)
    plan_by_dest = jnp.pad(
        send_plan[0, 0, 0:2].reshape(2, n, most).transpose(1, 0, 2),
        ((0, 0), (0, 6), (0, 128 - most)),
    )

    wide_rim = padded_2(heights, (("dy", 0), ("dx", 1)), 2)
    slope_x, slope_y = slopes(wide_rim[1:-1, 1:-1])
    fields = shading(slope_x, slope_y, albedo).astype(jnp.bfloat16)
    tiles, plans = gather_tiles(fields, plan_by_dest, n)

    lap_field = laplace(wide_rim)
    row_ids = jnp.arange(tile_rows + 2)
    col_ids = jnp.arange(tile_cols + 2)
    row_keep = ~(
        (row_ids == 0) & (lax.axis_index("dy") == 0)
        | (row_ids == tile_rows + 1) & (lax.axis_index("dy") == lax.axis_size("dy") - 1)
    )
    col_keep = ~(
        (col_ids == 0) & (lax.axis_index("dx") == 0)
        | (col_ids == tile_cols + 1) & (lax.axis_index("dx") == lax.axis_size("dx") - 1)
    )
    keep_mask = row_keep[:, None] & col_keep[None, :]
    smoothness_term = laplace(jnp.where(keep_mask, lap_field, 0.0))

    tile_grads, sums = render(plans, pick, used, light, tiles, resample, observed, most)
    grads, camera = scatter_sums(tile_grads, sums.reshape(n, crops // n, 8, size), n)

    coordinate = (jnp.arange(size, dtype=jnp.float32) - 0.5 * (size - 1)) / size
    plain = jnp.sum(camera, axis=-1)
    placed = jnp.sum(camera * coordinate, axis=-1)
    camera_model = jnp.stack(
        [
            plain[:, 0] / size,
            placed[:, 0] / size,
            plain[:, 1] / size,
            plain[:, 2] / size,
            placed[:, 2] / size,
            plain[:, 3] / size,
            plain[:, 4] / (size * size),
        ],
        axis=-1,
    )

    grad_x, grad_y = grads[0], grads[1]
    low_x, high_x = shifted(grad_x.astype(jnp.bfloat16), "dx", 1, 1)
    low_y, high_y = shifted(grad_y.astype(jnp.bfloat16), "dy", 0, 1)
    rim_x = jnp.concatenate([low_x.astype(jnp.float32), grad_x, high_x.astype(jnp.float32)], axis=1)
    rim_y = jnp.concatenate([low_y.astype(jnp.float32), grad_y, high_y.astype(jnp.float32)], axis=0)
    data_term_gradient = (rim_x[:, :-2] - rim_x[:, 2:]) * 0.5 + (rim_y[:-2] - rim_y[2:]) * 0.5
    height_gradient = data_term_gradient + SMOOTHING_WEIGHT * smoothness_term
    return (height_gradient, camera_model[None])


def solution(mesh):
    placed = (
        P("dy", "dx"),
        P("dy", "dx"),
        P(("dy", "dx"), None, None),
        P(("dy", "dx"), None, None, None),
        P("dx", None),
        P("dx", None),
        P("dx", None),
        P("dy", "dx", None, None),
        P("dy", "dx", None),
    )
    return jax.shard_map(
        per_device,
        mesh=mesh,
        in_specs=placed,
        out_specs=(P("dy", "dx"), P("dx", "dy", None)),
        check_vma=False,
    )
```

```python
import functools

import jax
import jax.numpy as jnp
from jax import lax
from jax.experimental import pallas as pl
from jax.experimental.pallas import tpu as pltpu
from jax.sharding import PartitionSpec as P

SMOOTHING_WEIGHT = 0.02
MESH = pl.DeviceIdType.MESH
VMEM_BYTES = 56 * 1024 * 1024


def sun_vectors(solar_azimuth, elevation):
    return jnp.stack(
        [
            jnp.cos(elevation) * jnp.cos(solar_azimuth),
            jnp.cos(elevation) * jnp.sin(solar_azimuth),
            jnp.sin(elevation),
        ]
    )


def bit_count(count):
    bits = count.bit_length() - 1
    assert 1 << bits == count
    return bits


def flipped(index, mask, bits):
    for bit in range(bits):
        if mask >> bit & 1:
            weight = 1 << bit
            index = index + weight * (1 - 2 * ((index // weight) % 2))
    return index


def bit_orders(bits):
    up = list(range(1, bits))
    return (up, up[::-1])


def all_masks(order):
    masks = [0]
    for bit in order:
        masks = masks + [mask | 1 << bit for mask in masks]
    return masks


def columns_as_rows(block, low):
    width = block.shape[1]
    if low:
        return jnp.transpose(block[:, :128])[:8]
    return jnp.transpose(block[:, width - 128 :])[120:]


def rows_as_columns(rows, low):
    empty = jnp.zeros((120, rows.shape[1]), rows.dtype)
    parts = [empty, rows] if low else [rows, empty]
    return jnp.transpose(jnp.concatenate(parts, axis=0))


def greet(n, n_dx, corners):
    me, across = lax.axis_index("dy"), lax.axis_index("dx")
    barrier = pltpu.get_barrier_semaphore()
    for step in range(1, n):
        pl.semaphore_signal(
            barrier, inc=1, device_id={"dy": lax.rem(me + step, n)}, device_id_type=MESH
        )
    for side in (1, n_dx - 1):
        for up in (0, 1, n - 1) if corners else (0,):
            pl.semaphore_signal(
                barrier,
                inc=1,
                device_id={"dy": lax.rem(me + up, n), "dx": lax.rem(across + side, n_dx)},
                device_id_type=MESH,
            )
    pl.semaphore_wait(barrier, n - 1 + (6 if corners else 2))


def gather_kernel(
    n,
    n_dx,
    copies,
    heights_ref,
    albedo_ref,
    plan_ref,
    out_ref,
    plans_ref,
    smooth_ref,
    own_ref,
    edges,
    row_rim,
    col_rim,
    corner_rim,
    wide,
    send,
    recv,
    psend,
    precv,
    hsend,
    hrecv,
    lsem,
):
    bits = bit_count(n)
    me, across = lax.axis_index("dy"), lax.axis_index("dx")
    tile_rows, tile_cols = heights_ref.shape
    half = tile_rows // 2
    heights = heights_ref[...]
    edges[0] = columns_as_rows(heights, True)
    edges[1] = columns_as_rows(heights, False)
    greet(n, n_dx, True)

    row_parts = (pl.ds(0, 8), pl.ds(tile_rows - 8, 8))
    col_parts = (pl.ds(0, 128), pl.ds(tile_cols - 128, 128))
    row_to = (lax.rem(me + n - 1, n), lax.rem(me + 1, n))
    col_to = (lax.rem(across + n_dx - 1, n_dx), lax.rem(across + 1, n_dx))
    halos = []

    def halo(source, target, device):
        c = len(halos)
        copy = pltpu.make_async_remote_copy(
            src_ref=source,
            dst_ref=target,
            send_sem=hsend.at[c],
            recv_sem=hrecv.at[c],
            device_id=device,
            device_id_type=MESH,
        )
        copy.start()
        halos.append(copy)

    for up in range(2):
        halo(edges.at[up], col_rim.at[up], {"dx": col_to[up]})
    for up in range(2):
        halo(heights_ref.at[row_parts[up]], row_rim.at[up], {"dy": row_to[up]})
    for up in range(2):
        for right in range(2):
            halo(
                heights_ref.at[row_parts[up], col_parts[right]],
                corner_rim.at[up * 2 + right],
                {"dy": row_to[up], "dx": col_to[right]},
            )
    for copy in halos:
        copy.wait_recv()

    top, bottom = row_rim[1], row_rim[0]
    wide[...] = jnp.zeros_like(wide)
    inner_rows, inner_cols = pl.ds(8, tile_rows), pl.ds(128, tile_cols)
    wide[inner_rows, inner_cols] = heights
    wide[0:8, inner_cols] = jnp.where(me > 0, top, 0.0)
    wide[pl.ds(8 + tile_rows, 8), inner_cols] = jnp.where(me < n - 1, bottom, 0.0)
    wide[inner_rows, 0:128] = jnp.where(across > 0, rows_as_columns(col_rim[1], True), 0.0)
    wide[inner_rows, pl.ds(128 + tile_cols, 128)] = jnp.where(
        across < n_dx - 1, rows_as_columns(col_rim[0], False), 0.0
    )
    for up in range(2):
        for right in range(2):
            inside = (me > 0 if up else me < n - 1) & (across > 0 if right else across < n_dx - 1)
            wide[
                pl.ds(0 if up else 8 + tile_rows, 8), pl.ds(0 if right else 128 + tile_cols, 128)
            ] = jnp.where(inside, corner_rim[up * 2 + right], 0.0)

    def inner(block):
        return block[8 : 8 + tile_rows, 128 : 128 + tile_cols]

    def around(block):
        rows_all, cols_all = block.shape
        return (
            pltpu.roll(block, 1, 0),
            pltpu.roll(block, rows_all - 1, 0),
            pltpu.roll(block, 1, 1),
            pltpu.roll(block, cols_all - 1, 1),
        )

    above, below, left, right = around(wide[...])
    slope_x = inner(right - left) * 0.5
    slope_y = inner(below - above) * 0.5
    up = albedo_ref[...] * lax.rsqrt(1.0 + slope_x * slope_x + slope_y * slope_y)
    own_ref[0] = (-slope_x * up).astype(own_ref.dtype)
    own_ref[1] = (-slope_y * up).astype(own_ref.dtype)
    own_ref[2] = up.astype(own_ref.dtype)

    number = iter(range(copies))

    def rows(part):
        return pl.ds(part * half, half)

    def make(mask, part, bit):
        tile = flipped(me, mask, bits)
        source = own_ref if mask == 0 else out_ref.at[tile]
        c = next(number)
        return pltpu.make_async_remote_copy(
            src_ref=source.at[:, rows(part), :],
            dst_ref=out_ref.at[tile, :, rows(part), :],
            send_sem=send.at[c],
            recv_sem=recv.at[c],
            device_id={"dy": flipped(me, 1 << bit, bits)},
            device_id_type=MESH,
        )

    orders = bit_orders(bits)
    started = []
    arriving = {}

    def forward(mask, part, over):
        copy = make(mask, part, over)
        copy.start()
        started.append(copy)
        arriving[(mask | 1 << over, part)] = copy

    def later(mask, order):
        seen = [k for k, bit in enumerate(order) if mask >> bit & 1]
        return order[(max(seen) + 1 if seen else 0) :]

    for position in range(bits - 1):
        for part, order in enumerate(orders):
            forward(0, part, order[position])
    plan_copies = []
    for step in range(1, n):
        to = lax.rem(me + step, n)
        copy = pltpu.make_async_remote_copy(
            src_ref=plan_ref.at[to],
            dst_ref=plans_ref.at[me],
            send_sem=psend.at[step - 1],
            recv_sem=precv.at[step - 1],
            device_id={"dy": to},
            device_id_type=MESH,
        )
        copy.start()
        plan_copies.append(copy)
    for part in range(2):
        forward(0, part, 0)
    local = pltpu.make_async_copy(own_ref, out_ref.at[me], lsem.at[0])
    local.start()
    local_plan = pltpu.make_async_copy(plan_ref.at[me], plans_ref.at[me], lsem.at[1])
    local_plan.start()

    center = wide[...]
    above, below, left, right = around(center)
    lap = above + below + left + right - 4.0 * center
    row = lax.broadcasted_iota(jnp.int32, (center.shape[0], 1), 0)
    col = lax.broadcasted_iota(jnp.int32, (1, center.shape[1]), 1)
    row_keep = ((row >= 8) | (me > 0)) & ((row < 8 + tile_rows) | (me < n - 1))
    col_keep = ((col >= 128) | (across > 0)) & ((col < 128 + tile_cols) | (across < n_dx - 1))
    lap = jnp.where(row_keep & col_keep, lap, 0.0)
    above, below, left, right = around(lap)
    smooth_ref[...] = SMOOTHING_WEIGHT * inner(above + below + left + right - 4.0 * lap)

    mask_lists = [all_masks(order)[1:] for order in orders]
    for position in range(len(mask_lists[0])):
        for part, order in enumerate(orders):
            mask = mask_lists[part][position]
            arriving[(mask, part)].wait_recv()
            for bit in later(mask, order):
                forward(mask, part, bit)
            forward(mask, part, 0)
    for (mask, part), copy in arriving.items():
        if mask & 1:
            copy.wait_recv()
    for copy in started:
        copy.wait_send()
    for copy in plan_copies:
        copy.wait()
    for copy in halos:
        copy.wait_send()
    local.wait()
    local_plan.wait()


def gather_tiles(heights, albedo, plan_by_dest, n, n_dx):
    copies = 2 * (n // 2 - 1) + n
    tile_rows, tile_cols = heights.shape
    vmem = pl.BlockSpec(memory_space=pltpu.VMEM)
    hbm = pl.BlockSpec(memory_space=pl.ANY)
    return pl.pallas_call(
        functools.partial(gather_kernel, n, n_dx, copies),
        out_shape=(
            jax.ShapeDtypeStruct((n, 3, tile_rows, tile_cols), jnp.bfloat16),
            jax.ShapeDtypeStruct(plan_by_dest.shape, plan_by_dest.dtype),
            jax.ShapeDtypeStruct(heights.shape, jnp.float32),
        ),
        in_specs=[vmem, vmem, hbm],
        out_specs=(hbm, hbm, vmem),
        scratch_shapes=[
            pltpu.VMEM((3, tile_rows, tile_cols), jnp.bfloat16),
            pltpu.VMEM((2, 8, tile_rows), jnp.float32),
            pltpu.VMEM((2, 8, tile_cols), jnp.float32),
            pltpu.VMEM((2, 8, tile_rows), jnp.float32),
            pltpu.VMEM((4, 8, 128), jnp.float32),
            pltpu.VMEM((tile_rows + 16, tile_cols + 256), jnp.float32),
            pltpu.SemaphoreType.DMA((copies,)),
            pltpu.SemaphoreType.DMA((copies,)),
            pltpu.SemaphoreType.DMA((n - 1,)),
            pltpu.SemaphoreType.DMA((n - 1,)),
            pltpu.SemaphoreType.DMA((8,)),
            pltpu.SemaphoreType.DMA((8,)),
            pltpu.SemaphoreType.DMA((2,)),
        ],
        compiler_params=pltpu.CompilerParams(
            collective_id=0, has_side_effects=True, vmem_limit_bytes=VMEM_BYTES
        ),
        name="gather_tiles",
    )(heights, albedo, plan_by_dest)


def render_kernel(
    plans, pick, used, light, tiles_ref, mats_ref, seen_ref, grads_ref, sums_ref, total
):
    tile, slot = pl.program_id(0), pl.program_id(1)
    most = pl.num_programs(1)
    step = tile * most + slot
    size = seen_ref.shape[-1]

    @pl.when(slot == 0)
    def _():
        total[...] = jnp.zeros_like(total)

    @pl.when(used[step] == 1)
    def _():
        image = pick[step]
        rows = pl.ds(pl.multiple_of(plans[tile, 0, slot], 128), size)
        cols = pl.ds(pl.multiple_of(plans[tile, 1, slot], 128), size)
        sun_x, sun_y, sun_z = light[0, image], light[1, image], light[2, image]
        gain = light[3, image]

        def field(k):
            return tiles_ref[0, k, rows, cols].astype(jnp.float32)

        shaded = (sun_x * field(0) + sun_y * field(1) + sun_z * field(2)).astype(jnp.bfloat16)
        first = jnp.dot(mats_ref[0, 0], shaded, preferred_element_type=jnp.float32)
        predicted = gain * lax.dot_general(
            first.astype(jnp.bfloat16),
            mats_ref[0, 1],
            (((1,), (1,)), ((), ())),
            preferred_element_type=jnp.float32,
        )
        residual = predicted - seen_ref[0].astype(jnp.float32)
        weighted = (gain * residual).astype(jnp.bfloat16)
        back = lax.dot_general(
            mats_ref[0, 0], weighted, (((0,), (0,)), ((), ())), preferred_element_type=jnp.float32
        ).astype(jnp.bfloat16)
        crop_grad = jnp.dot(back, mats_ref[0, 1], preferred_element_type=jnp.float32)

        col = lax.broadcasted_iota(jnp.int32, (1, size), 1)
        row = lax.broadcasted_iota(jnp.int32, (size, 1), 0)
        last = size - 1
        right = jnp.where(col == last, predicted, pltpu.roll(predicted, last, 1))
        left = jnp.where(col == 0, predicted, pltpu.roll(predicted, 1, 1))
        below = jnp.where(row == last, predicted, pltpu.roll(predicted, last, 0))
        above = jnp.where(row == 0, predicted, pltpu.roll(predicted, 1, 0))
        col_weight = jnp.where((col == 0) | (col == last), 1.0, 0.5)
        row_weight = jnp.where((row == 0) | (row == last), 1.0, 0.5)
        row_place = (row.astype(jnp.float32) - 0.5 * (size - 1)) / size
        by_u = residual * (right - left)
        by_v = residual * ((below - above) * row_weight)
        sums_ref[image, 0:1] = col_weight * jnp.sum(by_u, axis=0, keepdims=True)
        sums_ref[image, 1:2] = col_weight * jnp.sum(by_u * row_place, axis=0, keepdims=True)
        sums_ref[image, 2:3] = jnp.sum(by_v, axis=0, keepdims=True)
        sums_ref[image, 3:4] = jnp.sum(by_v * row_place, axis=0, keepdims=True)
        sums_ref[image, 4:5] = jnp.sum(residual * predicted, axis=0, keepdims=True)
        sums_ref[image, 5:8] = jnp.zeros((3, size), jnp.float32)

        fx, fy, fz = field(0), field(1), field(2)
        along = (sun_x * fx + sun_y * fy + sun_z * fz) / (fx * fx + fy * fy + fz * fz)
        scaled = crop_grad * fz
        total[0, rows, cols] += scaled * (fx * along - sun_x)
        total[1, rows, cols] += scaled * (fy * along - sun_y)

    @pl.when(slot == most - 1)
    def _():
        grads_ref[0] = total[...].astype(grads_ref.dtype)


def render(plans, pick, used, light, tiles, resample, observed, most):
    n, _, tile_rows, tile_cols = tiles.shape
    crops, size, _ = observed.shape

    def crop_at(t, j, plans, pick, used):
        return pick[t * most + j]

    def inner(plans, pick, used, light, *refs):
        render_kernel(plans, pick, used, light, *refs)

    return pl.pallas_call(
        inner,
        out_shape=(
            jax.ShapeDtypeStruct((n, 2, tile_rows, tile_cols), jnp.bfloat16),
            jax.ShapeDtypeStruct((crops, 8, size), jnp.float32),
        ),
        grid_spec=pltpu.PrefetchScalarGridSpec(
            num_scalar_prefetch=3,
            grid=(n, most),
            in_specs=[
                pl.BlockSpec(memory_space=pltpu.SMEM),
                pl.BlockSpec((1, 3, tile_rows, tile_cols), lambda t, j, *s: (t, 0, 0, 0)),
                pl.BlockSpec((1, 2, size, size), lambda t, j, *s: (crop_at(t, j, *s), 0, 0, 0)),
                pl.BlockSpec((1, size, size), lambda t, j, *s: (crop_at(t, j, *s), 0, 0)),
            ],
            out_specs=(
                pl.BlockSpec((1, 2, tile_rows, tile_cols), lambda t, j, *s: (t, 0, 0, 0)),
                pl.BlockSpec((crops, 8, size), lambda t, j, *s: (0, 0, 0)),
            ),
            scratch_shapes=[pltpu.VMEM((2, tile_rows, tile_cols), jnp.float32)],
        ),
        compiler_params=pltpu.CompilerParams(
            dimension_semantics=("arbitrary", "arbitrary"), vmem_limit_bytes=VMEM_BYTES
        ),
        name="render",
    )(plans, pick, used, light, tiles, resample, observed)


def scatter_kernel(
    n,
    n_dx,
    grads_ref,
    sums_ref,
    smooth_ref,
    height_ref,
    camera_ref,
    kept,
    first,
    later,
    out_ref,
    csums,
    edges,
    rims,
    send,
    recv,
    csend,
    crecv,
    hsend,
    hrecv,
    lsem,
):
    bits = bit_count(n)
    me, across = lax.axis_index("dy"), lax.axis_index("dx")
    tile_rows, tile_cols = height_ref.shape
    half = tile_rows // 2
    greet(n, n_dx, False)

    number = iter(range(send.shape[0]))
    started = []

    def push(source, target, bit):
        c = next(number)
        copy = pltpu.make_async_remote_copy(
            src_ref=source,
            dst_ref=target,
            send_sem=send.at[c],
            recv_sem=recv.at[c],
            device_id={"dy": flipped(me, 1 << bit, bits)},
            device_id_type=MESH,
        )
        copy.start()
        started.append(copy)
        return copy

    masks = [m << 1 for m in range(n // 2)][::-1]
    pair = {}
    for mask in masks:
        pair[mask] = push(grads_ref.at[flipped(me, mask + 1, bits)], first.at[mask >> 1], 0)
    loads = {}
    for mask in masks:
        loads[mask] = pltpu.make_async_copy(
            grads_ref.at[flipped(me, mask, bits)], kept.at[mask >> 1], lsem.at[mask >> 1]
        )
        loads[mask].start()
    camera_copies = []
    for step in range(1, n):
        to = lax.rem(me + step, n)
        copy = pltpu.make_async_remote_copy(
            src_ref=sums_ref.at[to],
            dst_ref=csums.at[step - 1],
            send_sem=csend.at[step - 1],
            recv_sem=crecv.at[step - 1],
            device_id={"dy": to},
            device_id_type=MESH,
        )
        copy.start()
        camera_copies.append(copy)

    orders = bit_orders(bits)
    places = iter(range(later.shape[0]))
    coming = {}

    def rows(part):
        return pl.ds(part * half, half)

    for mask in masks:
        loads[mask].wait()
        pair[mask].wait_recv()
        mine = kept[mask >> 1].astype(jnp.float32)
        both = mine + first[mask >> 1].astype(jnp.float32)
        if mask == 0:
            out_ref[...] = both
        else:
            first[mask >> 1] = both.astype(first.dtype)
            for part, order in enumerate(orders):
                if mask >> order[0] & 1:
                    at = next(places)
                    source = first.at[mask >> 1, :, rows(part), :]
                    copy = push(source, later.at[at], order[0])
                    coming[(part, mask ^ 1 << order[0])] = (copy, at)
    for stage in range(bits - 1):
        for part, order in enumerate(orders):
            landed = [(m, coming.pop((p, m))) for p, m in list(coming) if p == part]
            for mask, (copy, at) in landed:
                copy.wait_recv()
                add = later[at].astype(jnp.float32)
                if mask == 0:
                    out_ref[:, rows(part), :] += add
                else:
                    held = first[mask >> 1, :, rows(part), :].astype(jnp.float32)
                    first[mask >> 1, :, rows(part), :] = (held + add).astype(first.dtype)
                    bit = order[stage + 1]
                    if mask >> bit & 1:
                        to = next(places)
                        source = first.at[mask >> 1, :, rows(part), :]
                        sent = push(source, later.at[to], bit)
                        coming[(part, mask ^ 1 << bit)] = (sent, to)
    grad_x, grad_y = out_ref[0], out_ref[1]
    edges[0] = columns_as_rows(grad_x, True)
    edges[1] = columns_as_rows(grad_x, False)
    edges[2] = grad_y[:8]
    edges[3] = grad_y[tile_rows - 8 :]
    targets = (
        {"dx": lax.rem(across + n_dx - 1, n_dx)},
        {"dx": lax.rem(across + 1, n_dx)},
        {"dy": lax.rem(me + n - 1, n)},
        {"dy": lax.rem(me + 1, n)},
    )
    halos = []
    for c, device in enumerate(targets):
        copy = pltpu.make_async_remote_copy(
            src_ref=edges.at[c],
            dst_ref=rims.at[c],
            send_sem=hsend.at[c],
            recv_sem=hrecv.at[c],
            device_id=device,
            device_id_type=MESH,
        )
        copy.start()
        halos.append(copy)
    camera = sums_ref[me]
    for step in range(1, n):
        camera_copies[step - 1].wait()
        camera = camera + csums[step - 1]
    camera_ref[...] = camera
    for copy in started:
        copy.wait_send()
    for copy in halos:
        copy.wait()

    after_x = jnp.where(across < n_dx - 1, rows_as_columns(rims[0], False), 0.0)[:, 0:1]
    before_x = jnp.where(across > 0, rows_as_columns(rims[1], True), 0.0)[:, 127:128]
    after_y = jnp.where(me < n - 1, rims[2], 0.0)[0:1]
    before_y = jnp.where(me > 0, rims[3], 0.0)[7:8]
    row = lax.broadcasted_iota(jnp.int32, (tile_rows, 1), 0)
    col = lax.broadcasted_iota(jnp.int32, (1, tile_cols), 1)
    left = jnp.where(col == 0, before_x, pltpu.roll(grad_x, 1, 1))
    right = jnp.where(col == tile_cols - 1, after_x, pltpu.roll(grad_x, tile_cols - 1, 1))
    above = jnp.where(row == 0, before_y, pltpu.roll(grad_y, 1, 0))
    below = jnp.where(row == tile_rows - 1, after_y, pltpu.roll(grad_y, tile_rows - 1, 0))
    height_ref[...] = 0.5 * ((left - right) + (above - below)) + smooth_ref[...]


def scatter_sums(grads, sums, smooth, n, n_dx):
    _, parts, tile_rows, tile_cols = grads.shape
    assert tile_rows == tile_cols
    high = n // 2
    halves = 2 * (high - 1)
    copies = high + halves
    vmem = pl.BlockSpec(memory_space=pltpu.VMEM)
    return pl.pallas_call(
        functools.partial(scatter_kernel, n, n_dx),
        out_shape=(
            jax.ShapeDtypeStruct(smooth.shape, jnp.float32),
            jax.ShapeDtypeStruct(sums.shape[1:], jnp.float32),
        ),
        in_specs=[pl.BlockSpec(memory_space=pl.ANY), vmem, vmem],
        out_specs=(vmem, vmem),
        scratch_shapes=[
            pltpu.VMEM((high, parts, tile_rows, tile_cols), grads.dtype),
            pltpu.VMEM((high, parts, tile_rows, tile_cols), grads.dtype),
            pltpu.VMEM((halves, parts, tile_rows // 2, tile_cols), grads.dtype),
            pltpu.VMEM((parts, tile_rows, tile_cols), jnp.float32),
            pltpu.VMEM((n - 1,) + sums.shape[1:], jnp.float32),
            pltpu.VMEM((4, 8, tile_cols), jnp.float32),
            pltpu.VMEM((4, 8, tile_cols), jnp.float32),
            pltpu.SemaphoreType.DMA((copies,)),
            pltpu.SemaphoreType.DMA((copies,)),
            pltpu.SemaphoreType.DMA((n - 1,)),
            pltpu.SemaphoreType.DMA((n - 1,)),
            pltpu.SemaphoreType.DMA((4,)),
            pltpu.SemaphoreType.DMA((4,)),
            pltpu.SemaphoreType.DMA((high,)),
        ],
        compiler_params=pltpu.CompilerParams(
            collective_id=1, has_side_effects=True, vmem_limit_bytes=VMEM_BYTES
        ),
        name="scatter_sums",
    )(grads, sums, smooth)


def per_device(
    heights, albedo, observed, resample, exposure, sun_azimuth, sun_elevation, send_plan, recv_plan
):
    n, n_dx = lax.axis_size("dy"), lax.axis_size("dx")
    crops, size = observed.shape[0], observed.shape[-1]
    slot_count = send_plan.shape[-1]
    most = slot_count // n
    receive = recv_plan[0, 0]
    sun_table = sun_vectors(sun_azimuth[0], sun_elevation[0])
    light = jnp.concatenate([sun_table, jnp.exp(exposure)])
    slot_ids = jnp.arange(slot_count, dtype=jnp.int32)
    reached = jnp.where(receive[None, :] <= slot_ids[:, None], receive[None, :], -1)
    pick = jnp.argmax(reached, axis=1).astype(jnp.int32)
    used = (jnp.max(reached, axis=1) == slot_ids).astype(jnp.int32)
    plan_by_dest = jnp.pad(
        send_plan[0, 0, 0:2].reshape(2, n, most).transpose(1, 0, 2),
        ((0, 0), (0, 6), (0, 128 - most)),
    )

    tiles, plans, smooth = gather_tiles(heights, albedo, plan_by_dest, n, n_dx)
    tile_grads, sums = render(plans, pick, used, light, tiles, resample, observed, most)
    height_gradient, camera = scatter_sums(
        tile_grads, sums.reshape(n, crops // n, 8, size), smooth, n, n_dx
    )

    coordinate = (jnp.arange(size, dtype=jnp.float32) - 0.5 * (size - 1)) / size
    plain = jnp.sum(camera, axis=-1)
    placed = jnp.sum(camera * coordinate, axis=-1)
    camera_model = jnp.stack(
        [
            plain[:, 0] / size,
            placed[:, 0] / size,
            plain[:, 1] / size,
            plain[:, 2] / size,
            placed[:, 2] / size,
            plain[:, 3] / size,
            plain[:, 4] / (size * size),
        ],
        axis=-1,
    )

    return (height_gradient, camera_model[None])


def solution(mesh):
    placed = (
        P("dy", "dx"),
        P("dy", "dx"),
        P(("dy", "dx"), None, None),
        P(("dy", "dx"), None, None, None),
        P("dx", None),
        P("dx", None),
        P("dx", None),
        P("dy", "dx", None, None),
        P("dy", "dx", None),
    )
    return jax.shard_map(
        per_device,
        mesh=mesh,
        in_specs=placed,
        out_specs=(P("dy", "dx"), P("dx", "dy", None)),
        check_vma=False,
    )
```

```python
import functools

import jax
import jax.numpy as jnp
from jax import lax
from jax.experimental import pallas as pl
from jax.experimental.pallas import tpu as pltpu
from jax.sharding import PartitionSpec as P

SMOOTHING_WEIGHT = 0.02
MESH = pl.DeviceIdType.MESH
VMEM_BYTES = 56 * 1024 * 1024
HEIGHT_SCALE = 8191.0
FIELD_SCALE = 21844.0
RIM_ROWS = 16


def fixed_point(values, scale):
    return jnp.floor(values * scale + 0.5).astype(jnp.int32).astype(jnp.int16)


def sun_vectors(solar_azimuth, elevation):
    return jnp.stack(
        [
            jnp.cos(elevation) * jnp.cos(solar_azimuth),
            jnp.cos(elevation) * jnp.sin(solar_azimuth),
            jnp.sin(elevation),
        ]
    )


def bit_count(count):
    bits = count.bit_length() - 1
    assert 1 << bits == count
    return bits


def flipped(index, mask, bits):
    for bit in range(bits):
        if mask >> bit & 1:
            weight = 1 << bit
            index = index + weight * (1 - 2 * ((index // weight) % 2))
    return index


def bit_orders(bits):
    up = list(range(1, bits))
    return (up, up[::-1])


def all_masks(order):
    masks = [0]
    for bit in order:
        masks = masks + [mask | 1 << bit for mask in masks]
    return masks


def columns_as_rows(block, low):
    width = block.shape[1]
    if low:
        return jnp.transpose(block[:, :128])[:8]
    return jnp.transpose(block[:, width - 128 :])[120:]


def rows_as_columns(rows, low):
    empty = jnp.zeros((120, rows.shape[1]), rows.dtype)
    parts = [empty, rows] if low else [rows, empty]
    return jnp.transpose(jnp.concatenate(parts, axis=0))


def greet(n, n_dx, corners):
    me, across = lax.axis_index("dy"), lax.axis_index("dx")
    barrier = pltpu.get_barrier_semaphore()
    for step in range(1, n):
        pl.semaphore_signal(
            barrier, inc=1, device_id={"dy": lax.rem(me + step, n)}, device_id_type=MESH
        )
    for side in (1, n_dx - 1):
        for up in (0, 1, n - 1) if corners else (0,):
            pl.semaphore_signal(
                barrier,
                inc=1,
                device_id={"dy": lax.rem(me + up, n), "dx": lax.rem(across + side, n_dx)},
                device_id_type=MESH,
            )
    pl.semaphore_wait(barrier, n - 1 + (6 if corners else 2))


def gather_kernel(
    n,
    n_dx,
    copies,
    heights_ref,
    albedo_ref,
    plan_ref,
    out_ref,
    plans_ref,
    smooth_ref,
    own_ref,
    edges,
    row_rim,
    col_rim,
    corner_rim,
    wide,
    send,
    recv,
    psend,
    precv,
    hsend,
    hrecv,
    lsem,
):
    bits = bit_count(n)
    me, across = lax.axis_index("dy"), lax.axis_index("dx")
    tile_rows, tile_cols = heights_ref.shape
    cut = tile_rows + RIM_ROWS
    heights = heights_ref[...]
    own_ref[0:tile_rows] = fixed_point(heights, HEIGHT_SCALE)
    edges[0] = columns_as_rows(heights, True)
    edges[1] = columns_as_rows(heights, False)
    greet(n, n_dx, True)

    row_parts = (pl.ds(0, 8), pl.ds(tile_rows - 8, 8))
    col_parts = (pl.ds(0, 128), pl.ds(tile_cols - 128, 128))
    row_to = (lax.rem(me + n - 1, n), lax.rem(me + 1, n))
    col_to = (lax.rem(across + n_dx - 1, n_dx), lax.rem(across + 1, n_dx))
    halos = []

    def halo(source, target, device):
        c = len(halos)
        copy = pltpu.make_async_remote_copy(
            src_ref=source,
            dst_ref=target,
            send_sem=hsend.at[c],
            recv_sem=hrecv.at[c],
            device_id=device,
            device_id_type=MESH,
        )
        copy.start()
        halos.append(copy)

    for up in range(2):
        halo(edges.at[up], col_rim.at[up], {"dx": col_to[up]})
    for up in range(2):
        halo(heights_ref.at[row_parts[up]], row_rim.at[up], {"dy": row_to[up]})
    for up in range(2):
        for right in range(2):
            halo(
                heights_ref.at[row_parts[up], col_parts[right]],
                corner_rim.at[up * 2 + right],
                {"dy": row_to[up], "dx": col_to[right]},
            )
    for copy in halos:
        copy.wait_recv()

    top, bottom = row_rim[1], row_rim[0]
    wide[...] = jnp.zeros_like(wide)
    inner_rows, inner_cols = pl.ds(8, tile_rows), pl.ds(128, tile_cols)
    wide[inner_rows, inner_cols] = heights
    wide[0:8, inner_cols] = jnp.where(me > 0, top, 0.0)
    wide[pl.ds(8 + tile_rows, 8), inner_cols] = jnp.where(me < n - 1, bottom, 0.0)
    wide[inner_rows, 0:128] = jnp.where(across > 0, rows_as_columns(col_rim[1], True), 0.0)
    wide[inner_rows, pl.ds(128 + tile_cols, 128)] = jnp.where(
        across < n_dx - 1, rows_as_columns(col_rim[0], False), 0.0
    )
    for up in range(2):
        for right in range(2):
            inside = (me > 0 if up else me < n - 1) & (across > 0 if right else across < n_dx - 1)
            wide[
                pl.ds(0 if up else 8 + tile_rows, 8), pl.ds(0 if right else 128 + tile_cols, 128)
            ] = jnp.where(inside, corner_rim[up * 2 + right], 0.0)

    def inner(block):
        return block[8 : 8 + tile_rows, 128 : 128 + tile_cols]

    def around(block):
        rows_all, cols_all = block.shape
        return (
            pltpu.roll(block, 1, 0),
            pltpu.roll(block, rows_all - 1, 0),
            pltpu.roll(block, 1, 1),
            pltpu.roll(block, cols_all - 1, 1),
        )

    number = iter(range(copies))

    def rows(part):
        return pl.ds(part * cut, tile_rows if part else cut)

    def make(mask, part, bit):
        tile = flipped(me, mask, bits)
        source = own_ref if mask == 0 else out_ref.at[tile]
        c = next(number)
        return pltpu.make_async_remote_copy(
            src_ref=source.at[rows(part), :],
            dst_ref=out_ref.at[tile, rows(part), :],
            send_sem=send.at[c],
            recv_sem=recv.at[c],
            device_id={"dy": flipped(me, 1 << bit, bits)},
            device_id_type=MESH,
        )

    orders = bit_orders(bits)
    started = []
    arriving = {}

    def forward(mask, part, over):
        copy = make(mask, part, over)
        copy.start()
        started.append(copy)
        arriving[(mask | 1 << over, part)] = copy

    def later(mask, order):
        seen = [k for k, bit in enumerate(order) if mask >> bit & 1]
        return order[(max(seen) + 1 if seen else 0) :]

    place = lax.broadcasted_iota(jnp.int32, (RIM_ROWS, 1), 0)
    rim = jnp.where(place == 0, jnp.where(across < n_dx - 1, col_rim[0], 0.0)[0:1], 0.0)
    rim = jnp.where(place == 1, jnp.where(me < n - 1, row_rim[0], 0.0)[0:1], rim)
    rim = jnp.where(place == RIM_ROWS - 2, jnp.where(me > 0, row_rim[1], 0.0)[7:8], rim)
    rim = jnp.where(place == RIM_ROWS - 1, jnp.where(across > 0, col_rim[1], 0.0)[7:8], rim)
    own_ref[pl.ds(tile_rows, RIM_ROWS)] = fixed_point(rim, HEIGHT_SCALE)
    for position in range(bits - 1):
        forward(0, 0, orders[0][position])

    above, below, left, right = around(wide[...])
    slope_x = inner(right - left) * 0.5
    slope_y = inner(below - above) * 0.5
    up = albedo_ref[...] * lax.rsqrt(1.0 + slope_x * slope_x + slope_y * slope_y)
    own_ref[pl.ds(cut, tile_rows)] = fixed_point(up, FIELD_SCALE)
    for position in range(bits - 1):
        forward(0, 1, orders[1][position])
    plan_copies = []
    for step in range(1, n):
        to = lax.rem(me + step, n)
        copy = pltpu.make_async_remote_copy(
            src_ref=plan_ref.at[to],
            dst_ref=plans_ref.at[me],
            send_sem=psend.at[step - 1],
            recv_sem=precv.at[step - 1],
            device_id={"dy": to},
            device_id_type=MESH,
        )
        copy.start()
        plan_copies.append(copy)
    for part in range(2):
        forward(0, part, 0)
    local = pltpu.make_async_copy(own_ref, out_ref.at[me], lsem.at[0])
    local.start()
    local_plan = pltpu.make_async_copy(plan_ref.at[me], plans_ref.at[me], lsem.at[1])
    local_plan.start()

    center = wide[...]
    above, below, left, right = around(center)
    lap = above + below + left + right - 4.0 * center
    row = lax.broadcasted_iota(jnp.int32, (center.shape[0], 1), 0)
    col = lax.broadcasted_iota(jnp.int32, (1, center.shape[1]), 1)
    row_keep = ((row >= 8) | (me > 0)) & ((row < 8 + tile_rows) | (me < n - 1))
    col_keep = ((col >= 128) | (across > 0)) & ((col < 128 + tile_cols) | (across < n_dx - 1))
    lap = jnp.where(row_keep & col_keep, lap, 0.0)
    above, below, left, right = around(lap)
    smooth_ref[...] = SMOOTHING_WEIGHT * inner(above + below + left + right - 4.0 * lap)

    mask_lists = [all_masks(order)[1:] for order in orders]
    for position in range(len(mask_lists[0])):
        for part, order in enumerate(orders):
            mask = mask_lists[part][position]
            arriving[(mask, part)].wait_recv()
            for bit in later(mask, order):
                forward(mask, part, bit)
            forward(mask, part, 0)
    for (mask, part), copy in arriving.items():
        if mask & 1:
            copy.wait_recv()
    for copy in started:
        copy.wait_send()
    for copy in plan_copies:
        copy.wait()
    for copy in halos:
        copy.wait_send()
    local.wait()
    local_plan.wait()


def gather_tiles(heights, albedo, plan_by_dest, n, n_dx):
    copies = 2 * (n // 2 - 1) + n
    tile_rows, tile_cols = heights.shape
    vmem = pl.BlockSpec(memory_space=pltpu.VMEM)
    hbm = pl.BlockSpec(memory_space=pl.ANY)
    return pl.pallas_call(
        functools.partial(gather_kernel, n, n_dx, copies),
        out_shape=(
            jax.ShapeDtypeStruct((n, 2 * tile_rows + RIM_ROWS, tile_cols), jnp.int16),
            jax.ShapeDtypeStruct(plan_by_dest.shape, plan_by_dest.dtype),
            jax.ShapeDtypeStruct(heights.shape, jnp.float32),
        ),
        in_specs=[vmem, vmem, hbm],
        out_specs=(hbm, hbm, vmem),
        scratch_shapes=[
            pltpu.VMEM((2 * tile_rows + RIM_ROWS, tile_cols), jnp.int16),
            pltpu.VMEM((2, 8, tile_rows), jnp.float32),
            pltpu.VMEM((2, 8, tile_cols), jnp.float32),
            pltpu.VMEM((2, 8, tile_rows), jnp.float32),
            pltpu.VMEM((4, 8, 128), jnp.float32),
            pltpu.VMEM((tile_rows + 16, tile_cols + 256), jnp.float32),
            pltpu.SemaphoreType.DMA((copies,)),
            pltpu.SemaphoreType.DMA((copies,)),
            pltpu.SemaphoreType.DMA((n - 1,)),
            pltpu.SemaphoreType.DMA((n - 1,)),
            pltpu.SemaphoreType.DMA((8,)),
            pltpu.SemaphoreType.DMA((8,)),
            pltpu.SemaphoreType.DMA((2,)),
        ],
        compiler_params=pltpu.CompilerParams(
            collective_id=0, has_side_effects=True, vmem_limit_bytes=VMEM_BYTES
        ),
        name="gather_tiles",
    )(heights, albedo, plan_by_dest)


def render_kernel(
    plans, pick, used, light, tile_ref, mats_ref, seen_ref, grads_ref, sums_ref, total, fields
):
    tile, slot = pl.program_id(0), pl.program_id(1)
    most = pl.num_programs(1)
    step = tile * most + slot
    size = seen_ref.shape[-1]

    @pl.when(slot == 0)
    def _():
        total[...] = jnp.zeros_like(total)
        _, tile_rows, tile_cols = fields.shape
        ahead = tile_rows + RIM_ROWS

        def real(first, count):
            return tile_ref[0, pl.ds(first, count)].astype(jnp.int32).astype(jnp.float32)

        heights = real(0, tile_rows)
        rim = real(tile_rows, RIM_ROWS)
        side = RIM_ROWS // 2
        gap = jnp.zeros((128 - RIM_ROWS, tile_cols), jnp.float32)
        sides = jnp.transpose(jnp.concatenate([rim[:side], gap, rim[side:]], axis=0))
        across = jnp.concatenate([heights, sides], axis=1)
        right = pltpu.roll(across, tile_cols + 127, 1)[:, :tile_cols]
        left = pltpu.roll(across, 1, 1)[:, :tile_cols]
        line = lax.broadcasted_iota(jnp.int32, (tile_rows, 1), 0)
        above = jnp.where(line == 0, rim[RIM_ROWS - 2 : RIM_ROWS - 1], pltpu.roll(heights, 1, 0))
        below = jnp.where(line == tile_rows - 1, rim[1:2], pltpu.roll(heights, tile_rows - 1, 0))
        up = real(ahead, tile_rows) * (1.0 / FIELD_SCALE)
        slope_up = up * (0.5 / HEIGHT_SCALE)
        fields[0] = (left - right) * slope_up
        fields[1] = (above - below) * slope_up
        fields[2] = up

    @pl.when(used[step] == 1)
    def _():
        image = pick[step]
        rows = pl.ds(pl.multiple_of(plans[tile, 0, slot], 128), size)
        cols = pl.ds(pl.multiple_of(plans[tile, 1, slot], 128), size)
        sun_x, sun_y, sun_z = light[0, image], light[1, image], light[2, image]
        gain = light[3, image]

        def field(k):
            return fields[k, rows, cols]

        shaded = (sun_x * field(0) + sun_y * field(1) + sun_z * field(2)).astype(jnp.bfloat16)
        first = jnp.dot(mats_ref[0, 0], shaded, preferred_element_type=jnp.float32)
        predicted = gain * lax.dot_general(
            first.astype(jnp.bfloat16),
            mats_ref[0, 1],
            (((1,), (1,)), ((), ())),
            preferred_element_type=jnp.float32,
        )
        residual = predicted - seen_ref[0].astype(jnp.float32)
        weighted = (gain * residual).astype(jnp.bfloat16)
        back = lax.dot_general(
            mats_ref[0, 0], weighted, (((0,), (0,)), ((), ())), preferred_element_type=jnp.float32
        ).astype(jnp.bfloat16)
        crop_grad = jnp.dot(back, mats_ref[0, 1], preferred_element_type=jnp.float32)

        col = lax.broadcasted_iota(jnp.int32, (1, size), 1)
        row = lax.broadcasted_iota(jnp.int32, (size, 1), 0)
        last = size - 1
        right = jnp.where(col == last, predicted, pltpu.roll(predicted, last, 1))
        left = jnp.where(col == 0, predicted, pltpu.roll(predicted, 1, 1))
        below = jnp.where(row == last, predicted, pltpu.roll(predicted, last, 0))
        above = jnp.where(row == 0, predicted, pltpu.roll(predicted, 1, 0))
        col_weight = jnp.where((col == 0) | (col == last), 1.0, 0.5)
        row_place = (row.astype(jnp.float32) - 0.5 * (size - 1)) / size
        by_u = residual * (right - left)
        by_v = residual * (below - above)
        ends = 0.5 * (by_v[0:1] + by_v[last:])
        tilt = 0.5 * (0.5 * (size - 1) / size) * (by_v[last:] - by_v[0:1])
        sums_ref[image, 0:1] = col_weight * jnp.sum(by_u, axis=0, keepdims=True)
        sums_ref[image, 1:2] = col_weight * jnp.sum(by_u * row_place, axis=0, keepdims=True)
        sums_ref[image, 2:3] = 0.5 * jnp.sum(by_v, axis=0, keepdims=True) + ends
        sums_ref[image, 3:4] = 0.5 * jnp.sum(by_v * row_place, axis=0, keepdims=True) + tilt
        sums_ref[image, 4:5] = jnp.sum(residual * predicted, axis=0, keepdims=True)
        sums_ref[image, 5:8] = jnp.zeros((3, size), jnp.float32)

        fx, fy, fz = field(0), field(1), field(2)
        along = (sun_x * fx + sun_y * fy + sun_z * fz) * pl.reciprocal(
            fx * fx + fy * fy + fz * fz, approx=True
        )
        scaled = crop_grad * fz
        total[0, rows, cols] += scaled * (fx * along - sun_x)
        total[1, rows, cols] += scaled * (fy * along - sun_y)

    @pl.when(slot == most - 1)
    def _():
        grads_ref[0] = total[...].astype(grads_ref.dtype)


def render(plans, pick, used, light, tiles, resample, observed, most):
    n, packed_rows, tile_cols = tiles.shape
    tile_rows = (packed_rows - RIM_ROWS) // 2
    crops, size, _ = observed.shape

    def crop_at(t, j, plans, pick, used):
        return pick[t * most + j]

    def inner(plans, pick, used, light, *refs):
        render_kernel(plans, pick, used, light, *refs)

    return pl.pallas_call(
        inner,
        out_shape=(
            jax.ShapeDtypeStruct((n, 2, tile_rows, tile_cols), jnp.bfloat16),
            jax.ShapeDtypeStruct((crops, 8, size), jnp.float32),
        ),
        grid_spec=pltpu.PrefetchScalarGridSpec(
            num_scalar_prefetch=3,
            grid=(n, most),
            in_specs=[
                pl.BlockSpec(memory_space=pltpu.SMEM),
                pl.BlockSpec((1, packed_rows, tile_cols), lambda t, j, *s: (t, 0, 0)),
                pl.BlockSpec((1, 2, size, size), lambda t, j, *s: (crop_at(t, j, *s), 0, 0, 0)),
                pl.BlockSpec((1, size, size), lambda t, j, *s: (crop_at(t, j, *s), 0, 0)),
            ],
            out_specs=(
                pl.BlockSpec((1, 2, tile_rows, tile_cols), lambda t, j, *s: (t, 0, 0, 0)),
                pl.BlockSpec((crops, 8, size), lambda t, j, *s: (0, 0, 0)),
            ),
            scratch_shapes=[
                pltpu.VMEM((2, tile_rows, tile_cols), jnp.float32),
                pltpu.VMEM((3, tile_rows, tile_cols), jnp.float32),
            ],
        ),
        compiler_params=pltpu.CompilerParams(
            dimension_semantics=("arbitrary", "arbitrary"), vmem_limit_bytes=VMEM_BYTES
        ),
        name="render",
    )(plans, pick, used, light, tiles, resample, observed)


def scatter_kernel(
    n,
    n_dx,
    grads_ref,
    sums_ref,
    smooth_ref,
    height_ref,
    camera_ref,
    kept,
    first,
    later,
    out_ref,
    csums,
    edges,
    rims,
    send,
    recv,
    csend,
    crecv,
    hsend,
    hrecv,
    lsem,
):
    bits = bit_count(n)
    me, across = lax.axis_index("dy"), lax.axis_index("dx")
    tile_rows, tile_cols = height_ref.shape
    half = tile_rows // 2
    greet(n, n_dx, False)

    number = iter(range(send.shape[0]))
    started = []

    def push(source, target, bit):
        c = next(number)
        copy = pltpu.make_async_remote_copy(
            src_ref=source,
            dst_ref=target,
            send_sem=send.at[c],
            recv_sem=recv.at[c],
            device_id={"dy": flipped(me, 1 << bit, bits)},
            device_id_type=MESH,
        )
        copy.start()
        started.append(copy)
        return copy

    masks = [m << 1 for m in range(n // 2)][::-1]
    pair = {}

    def push_pair(mask):
        pair[mask] = push(grads_ref.at[flipped(me, mask + 1, bits)], first.at[mask >> 1], 0)

    push_pair(masks[0])
    loads = {}
    for mask in masks:
        loads[mask] = pltpu.make_async_copy(
            grads_ref.at[flipped(me, mask, bits)], kept.at[mask >> 1], lsem.at[mask >> 1]
        )
        loads[mask].start()
    camera_copies = []
    for step in range(1, n):
        to = lax.rem(me + step, n)
        copy = pltpu.make_async_remote_copy(
            src_ref=sums_ref.at[to],
            dst_ref=csums.at[step - 1],
            send_sem=csend.at[step - 1],
            recv_sem=crecv.at[step - 1],
            device_id={"dy": to},
            device_id_type=MESH,
        )
        copy.start()
        camera_copies.append(copy)

    orders = bit_orders(bits)
    places = iter(range(later.shape[0]))
    coming = {}

    def rows(part):
        return pl.ds(part * half, half)

    for mask in masks:
        loads[mask].wait()
        pair[mask].wait_recv()
        if mask:
            push_pair(mask - 2)
        mine = kept[mask >> 1].astype(jnp.float32)
        both = mine + first[mask >> 1].astype(jnp.float32)
        if mask == 0:
            out_ref[...] = both
        else:
            first[mask >> 1] = both.astype(first.dtype)
            for part, order in enumerate(orders):
                if mask >> order[0] & 1:
                    at = next(places)
                    source = first.at[mask >> 1, :, rows(part), :]
                    copy = push(source, later.at[at], order[0])
                    coming[(part, mask ^ 1 << order[0])] = (copy, at)
    for stage in range(bits - 1):
        for part, order in enumerate(orders):
            landed = [(m, coming.pop((p, m))) for p, m in list(coming) if p == part]
            for mask, (copy, at) in landed:
                copy.wait_recv()
                add = later[at].astype(jnp.float32)
                if mask == 0:
                    out_ref[:, rows(part), :] += add
                else:
                    held = first[mask >> 1, :, rows(part), :].astype(jnp.float32)
                    first[mask >> 1, :, rows(part), :] = (held + add).astype(first.dtype)
                    bit = order[stage + 1]
                    if mask >> bit & 1:
                        to = next(places)
                        source = first.at[mask >> 1, :, rows(part), :]
                        sent = push(source, later.at[to], bit)
                        coming[(part, mask ^ 1 << bit)] = (sent, to)
    grad_x, grad_y = out_ref[0], out_ref[1]
    edges[0] = columns_as_rows(grad_x, True)
    edges[1] = columns_as_rows(grad_x, False)
    edges[2] = grad_y[:8]
    edges[3] = grad_y[tile_rows - 8 :]
    targets = (
        {"dx": lax.rem(across + n_dx - 1, n_dx)},
        {"dx": lax.rem(across + 1, n_dx)},
        {"dy": lax.rem(me + n - 1, n)},
        {"dy": lax.rem(me + 1, n)},
    )
    halos = []
    for c, device in enumerate(targets):
        copy = pltpu.make_async_remote_copy(
            src_ref=edges.at[c],
            dst_ref=rims.at[c],
            send_sem=hsend.at[c],
            recv_sem=hrecv.at[c],
            device_id=device,
            device_id_type=MESH,
        )
        copy.start()
        halos.append(copy)
    camera = sums_ref[me]
    for step in range(1, n):
        camera_copies[step - 1].wait()
        camera = camera + csums[step - 1]
    camera_ref[...] = camera
    for copy in started:
        copy.wait_send()
    for copy in halos:
        copy.wait()

    after_x = jnp.where(across < n_dx - 1, rows_as_columns(rims[0], False), 0.0)[:, 0:1]
    before_x = jnp.where(across > 0, rows_as_columns(rims[1], True), 0.0)[:, 127:128]
    after_y = jnp.where(me < n - 1, rims[2], 0.0)[0:1]
    before_y = jnp.where(me > 0, rims[3], 0.0)[7:8]
    row = lax.broadcasted_iota(jnp.int32, (tile_rows, 1), 0)
    col = lax.broadcasted_iota(jnp.int32, (1, tile_cols), 1)
    left = jnp.where(col == 0, before_x, pltpu.roll(grad_x, 1, 1))
    right = jnp.where(col == tile_cols - 1, after_x, pltpu.roll(grad_x, tile_cols - 1, 1))
    above = jnp.where(row == 0, before_y, pltpu.roll(grad_y, 1, 0))
    below = jnp.where(row == tile_rows - 1, after_y, pltpu.roll(grad_y, tile_rows - 1, 0))
    height_ref[...] = 0.5 * ((left - right) + (above - below)) + smooth_ref[...]


def scatter_sums(grads, sums, smooth, n, n_dx):
    _, parts, tile_rows, tile_cols = grads.shape
    assert tile_rows == tile_cols
    high = n // 2
    halves = 2 * (high - 1)
    copies = high + halves
    vmem = pl.BlockSpec(memory_space=pltpu.VMEM)
    return pl.pallas_call(
        functools.partial(scatter_kernel, n, n_dx),
        out_shape=(
            jax.ShapeDtypeStruct(smooth.shape, jnp.float32),
            jax.ShapeDtypeStruct(sums.shape[1:], jnp.float32),
        ),
        in_specs=[pl.BlockSpec(memory_space=pl.ANY), vmem, vmem],
        out_specs=(vmem, vmem),
        scratch_shapes=[
            pltpu.VMEM((high, parts, tile_rows, tile_cols), grads.dtype),
            pltpu.VMEM((high, parts, tile_rows, tile_cols), grads.dtype),
            pltpu.VMEM((halves, parts, tile_rows // 2, tile_cols), grads.dtype),
            pltpu.VMEM((parts, tile_rows, tile_cols), jnp.float32),
            pltpu.VMEM((n - 1,) + sums.shape[1:], jnp.float32),
            pltpu.VMEM((4, 8, tile_cols), jnp.float32),
            pltpu.VMEM((4, 8, tile_cols), jnp.float32),
            pltpu.SemaphoreType.DMA((copies,)),
            pltpu.SemaphoreType.DMA((copies,)),
            pltpu.SemaphoreType.DMA((n - 1,)),
            pltpu.SemaphoreType.DMA((n - 1,)),
            pltpu.SemaphoreType.DMA((4,)),
            pltpu.SemaphoreType.DMA((4,)),
            pltpu.SemaphoreType.DMA((high,)),
        ],
        compiler_params=pltpu.CompilerParams(
            collective_id=1, has_side_effects=True, vmem_limit_bytes=VMEM_BYTES
        ),
        name="scatter_sums",
    )(grads, sums, smooth)


def per_device(
    heights, albedo, observed, resample, exposure, sun_azimuth, sun_elevation, send_plan, recv_plan
):
    n, n_dx = lax.axis_size("dy"), lax.axis_size("dx")
    crops, size = observed.shape[0], observed.shape[-1]
    slot_count = send_plan.shape[-1]
    most = slot_count // n
    receive = recv_plan[0, 0]
    sun_table = sun_vectors(sun_azimuth[0], sun_elevation[0])
    light = jnp.concatenate([sun_table, jnp.exp(exposure)])
    slot_ids = jnp.arange(slot_count, dtype=jnp.int32)
    reached = jnp.where(receive[None, :] <= slot_ids[:, None], receive[None, :], -1)
    pick = jnp.argmax(reached, axis=1).astype(jnp.int32)
    used = (jnp.max(reached, axis=1) == slot_ids).astype(jnp.int32)
    plan_by_dest = jnp.pad(
        send_plan[0, 0, 0:2].reshape(2, n, most).transpose(1, 0, 2),
        ((0, 0), (0, 6), (0, 128 - most)),
    )

    tiles, plans, smooth = gather_tiles(heights, albedo, plan_by_dest, n, n_dx)
    tile_grads, sums = render(plans, pick, used, light, tiles, resample, observed, most)
    height_gradient, camera = scatter_sums(
        tile_grads, sums.reshape(n, crops // n, 8, size), smooth, n, n_dx
    )

    coordinate = (jnp.arange(size, dtype=jnp.float32) - 0.5 * (size - 1)) / size
    plain = jnp.sum(camera, axis=-1)
    placed = jnp.sum(camera * coordinate, axis=-1)
    camera_model = jnp.stack(
        [
            plain[:, 0] / size,
            placed[:, 0] / size,
            plain[:, 1] / size,
            plain[:, 2] / size,
            placed[:, 2] / size,
            plain[:, 3] / size,
            plain[:, 4] / (size * size),
        ],
        axis=-1,
    )

    return (height_gradient, camera_model[None])


def solution(mesh):
    placed = (
        P("dy", "dx"),
        P("dy", "dx"),
        P(("dy", "dx"), None, None),
        P(("dy", "dx"), None, None, None),
        P("dx", None),
        P("dx", None),
        P("dx", None),
        P("dy", "dx", None, None),
        P("dy", "dx", None),
    )
    return jax.shard_map(
        per_device,
        mesh=mesh,
        in_specs=placed,
        out_specs=(P("dy", "dx"), P("dx", "dy", None)),
        check_vma=False,
    )
```

```python
import functools

import jax
import jax.numpy as jnp
from jax import lax
from jax.experimental import pallas as pl
from jax.experimental.pallas import tpu as pltpu
from jax.sharding import PartitionSpec as P

SMOOTHING_WEIGHT = 0.02
MESH = pl.DeviceIdType.MESH
VMEM_BYTES = 56 * 1024 * 1024
HEIGHT_SCALE = 8191.0
FIELD_SCALE = 21844.0
RIM_ROWS = 16


def fixed_point(values, scale):
    return jnp.floor(values * scale + 0.5).astype(jnp.int32).astype(jnp.int16)


def sun_vectors(solar_azimuth, elevation):
    return jnp.stack(
        [
            jnp.cos(elevation) * jnp.cos(solar_azimuth),
            jnp.cos(elevation) * jnp.sin(solar_azimuth),
            jnp.sin(elevation),
        ]
    )


def bit_count(count):
    bits = count.bit_length() - 1
    assert 1 << bits == count
    return bits


def flipped(index, mask, bits):
    for bit in range(bits):
        if mask >> bit & 1:
            weight = 1 << bit
            index = index + weight * (1 - 2 * ((index // weight) % 2))
    return index


def bit_orders(bits):
    up = list(range(1, bits))
    return (up, up[::-1])


def all_masks(order):
    masks = [0]
    for bit in order:
        masks = masks + [mask | 1 << bit for mask in masks]
    return masks


def columns_as_rows(block, low):
    width = block.shape[1]
    if low:
        return jnp.transpose(block[:, :128])[:8]
    return jnp.transpose(block[:, width - 128 :])[120:]


def rows_as_columns(rows, low):
    empty = jnp.zeros((120, rows.shape[1]), rows.dtype)
    parts = [empty, rows] if low else [rows, empty]
    return jnp.transpose(jnp.concatenate(parts, axis=0))


def greet(n, n_dx, corners):
    me, across = lax.axis_index("dy"), lax.axis_index("dx")
    barrier = pltpu.get_barrier_semaphore()
    for step in range(1, n):
        pl.semaphore_signal(
            barrier, inc=1, device_id={"dy": lax.rem(me + step, n)}, device_id_type=MESH
        )
    for side in (1, n_dx - 1):
        for up in (0, 1, n - 1) if corners else (0,):
            pl.semaphore_signal(
                barrier,
                inc=1,
                device_id={"dy": lax.rem(me + up, n), "dx": lax.rem(across + side, n_dx)},
                device_id_type=MESH,
            )
    pl.semaphore_wait(barrier, n - 1 + (6 if corners else 2))


def gather_kernel(
    n,
    n_dx,
    copies,
    heights_ref,
    albedo_ref,
    plan_ref,
    out_ref,
    plans_ref,
    smooth_ref,
    own_ref,
    edges,
    row_rim,
    col_rim,
    corner_rim,
    wide,
    send,
    recv,
    psend,
    precv,
    hsend,
    hrecv,
    lsem,
):
    bits = bit_count(n)
    me, across = lax.axis_index("dy"), lax.axis_index("dx")
    tile_rows, tile_cols = heights_ref.shape
    cut = tile_rows + RIM_ROWS
    heights = heights_ref[...]
    own_ref[0:tile_rows] = fixed_point(heights, HEIGHT_SCALE)
    edges[0] = columns_as_rows(heights, True)
    edges[1] = columns_as_rows(heights, False)
    greet(n, n_dx, True)

    row_parts = (pl.ds(0, 8), pl.ds(tile_rows - 8, 8))
    col_parts = (pl.ds(0, 128), pl.ds(tile_cols - 128, 128))
    row_to = (lax.rem(me + n - 1, n), lax.rem(me + 1, n))
    col_to = (lax.rem(across + n_dx - 1, n_dx), lax.rem(across + 1, n_dx))
    halos = []

    def halo(source, target, device):
        c = len(halos)
        copy = pltpu.make_async_remote_copy(
            src_ref=source,
            dst_ref=target,
            send_sem=hsend.at[c],
            recv_sem=hrecv.at[c],
            device_id=device,
            device_id_type=MESH,
        )
        copy.start()
        halos.append(copy)

    for up in range(2):
        halo(edges.at[up], col_rim.at[up], {"dx": col_to[up]})
    for up in range(2):
        halo(heights_ref.at[row_parts[up]], row_rim.at[up], {"dy": row_to[up]})
    for up in range(2):
        for right in range(2):
            halo(
                heights_ref.at[row_parts[up], col_parts[right]],
                corner_rim.at[up * 2 + right],
                {"dy": row_to[up], "dx": col_to[right]},
            )
    for copy in halos:
        copy.wait_recv()

    top, bottom = row_rim[1], row_rim[0]
    wide[...] = jnp.zeros_like(wide)
    inner_rows, inner_cols = pl.ds(8, tile_rows), pl.ds(128, tile_cols)
    wide[inner_rows, inner_cols] = heights
    wide[0:8, inner_cols] = jnp.where(me > 0, top, 0.0)
    wide[pl.ds(8 + tile_rows, 8), inner_cols] = jnp.where(me < n - 1, bottom, 0.0)
    wide[inner_rows, 0:128] = jnp.where(across > 0, rows_as_columns(col_rim[1], True), 0.0)
    wide[inner_rows, pl.ds(128 + tile_cols, 128)] = jnp.where(
        across < n_dx - 1, rows_as_columns(col_rim[0], False), 0.0
    )
    for up in range(2):
        for right in range(2):
            inside = (me > 0 if up else me < n - 1) & (across > 0 if right else across < n_dx - 1)
            wide[
                pl.ds(0 if up else 8 + tile_rows, 8), pl.ds(0 if right else 128 + tile_cols, 128)
            ] = jnp.where(inside, corner_rim[up * 2 + right], 0.0)

    def inner(block):
        return block[8 : 8 + tile_rows, 128 : 128 + tile_cols]

    def around(block):
        rows_all, cols_all = block.shape
        return (
            pltpu.roll(block, 1, 0),
            pltpu.roll(block, rows_all - 1, 0),
            pltpu.roll(block, 1, 1),
            pltpu.roll(block, cols_all - 1, 1),
        )

    number = iter(range(copies))

    def rows(part):
        return pl.ds(part * cut, tile_rows if part else cut)

    def make(mask, part, bit):
        tile = flipped(me, mask, bits)
        source = own_ref if mask == 0 else out_ref.at[tile]
        c = next(number)
        return pltpu.make_async_remote_copy(
            src_ref=source.at[rows(part), :],
            dst_ref=out_ref.at[tile, rows(part), :],
            send_sem=send.at[c],
            recv_sem=recv.at[c],
            device_id={"dy": flipped(me, 1 << bit, bits)},
            device_id_type=MESH,
        )

    orders = bit_orders(bits)
    started = []
    arriving = {}

    def forward(mask, part, over):
        copy = make(mask, part, over)
        copy.start()
        started.append(copy)
        arriving[(mask | 1 << over, part)] = copy

    def later(mask, order):
        seen = [k for k, bit in enumerate(order) if mask >> bit & 1]
        return order[(max(seen) + 1 if seen else 0) :]

    place = lax.broadcasted_iota(jnp.int32, (RIM_ROWS, 1), 0)
    rim = jnp.where(place == 0, jnp.where(across < n_dx - 1, col_rim[0], 0.0)[0:1], 0.0)
    rim = jnp.where(place == 1, jnp.where(me < n - 1, row_rim[0], 0.0)[0:1], rim)
    rim = jnp.where(place == RIM_ROWS - 2, jnp.where(me > 0, row_rim[1], 0.0)[7:8], rim)
    rim = jnp.where(place == RIM_ROWS - 1, jnp.where(across > 0, col_rim[1], 0.0)[7:8], rim)
    own_ref[pl.ds(tile_rows, RIM_ROWS)] = fixed_point(rim, HEIGHT_SCALE)
    for position in range(bits - 1):
        forward(0, 0, orders[0][position])

    above, below, left, right = around(wide[...])
    slope_x = inner(right - left) * 0.5
    slope_y = inner(below - above) * 0.5
    up = albedo_ref[...] * lax.rsqrt(1.0 + slope_x * slope_x + slope_y * slope_y)
    own_ref[pl.ds(cut, tile_rows)] = fixed_point(up, FIELD_SCALE)
    for position in range(bits - 1):
        forward(0, 1, orders[1][position])
    plan_copies = []
    for step in range(1, n):
        to = lax.rem(me + step, n)
        copy = pltpu.make_async_remote_copy(
            src_ref=plan_ref.at[to],
            dst_ref=plans_ref.at[me],
            send_sem=psend.at[step - 1],
            recv_sem=precv.at[step - 1],
            device_id={"dy": to},
            device_id_type=MESH,
        )
        copy.start()
        plan_copies.append(copy)
    for part in range(2):
        forward(0, part, 0)
    local = pltpu.make_async_copy(own_ref, out_ref.at[me], lsem.at[0])
    local.start()
    local_plan = pltpu.make_async_copy(plan_ref.at[me], plans_ref.at[me], lsem.at[1])
    local_plan.start()

    center = wide[...]
    above, below, left, right = around(center)
    lap = above + below + left + right - 4.0 * center
    row = lax.broadcasted_iota(jnp.int32, (center.shape[0], 1), 0)
    col = lax.broadcasted_iota(jnp.int32, (1, center.shape[1]), 1)
    row_keep = ((row >= 8) | (me > 0)) & ((row < 8 + tile_rows) | (me < n - 1))
    col_keep = ((col >= 128) | (across > 0)) & ((col < 128 + tile_cols) | (across < n_dx - 1))
    lap = jnp.where(row_keep & col_keep, lap, 0.0)
    above, below, left, right = around(lap)
    smooth_ref[...] = SMOOTHING_WEIGHT * inner(above + below + left + right - 4.0 * lap)

    mask_lists = [all_masks(order)[1:] for order in orders]
    for position in range(len(mask_lists[0])):
        for part, order in enumerate(orders):
            mask = mask_lists[part][position]
            arriving[(mask, part)].wait_recv()
            for bit in later(mask, order):
                forward(mask, part, bit)
            forward(mask, part, 0)
    for (mask, part), copy in arriving.items():
        if mask & 1:
            copy.wait_recv()
    for copy in started:
        copy.wait_send()
    for copy in plan_copies:
        copy.wait()
    for copy in halos:
        copy.wait_send()
    local.wait()
    local_plan.wait()


def gather_tiles(heights, albedo, plan_by_dest, n, n_dx):
    copies = 2 * (n // 2 - 1) + n
    tile_rows, tile_cols = heights.shape
    vmem = pl.BlockSpec(memory_space=pltpu.VMEM)
    hbm = pl.BlockSpec(memory_space=pl.ANY)
    return pl.pallas_call(
        functools.partial(gather_kernel, n, n_dx, copies),
        out_shape=(
            jax.ShapeDtypeStruct((n, 2 * tile_rows + RIM_ROWS, tile_cols), jnp.int16),
            jax.ShapeDtypeStruct(plan_by_dest.shape, plan_by_dest.dtype),
            jax.ShapeDtypeStruct(heights.shape, jnp.float32),
        ),
        in_specs=[vmem, vmem, hbm],
        out_specs=(hbm, hbm, vmem),
        scratch_shapes=[
            pltpu.VMEM((2 * tile_rows + RIM_ROWS, tile_cols), jnp.int16),
            pltpu.VMEM((2, 8, tile_rows), jnp.float32),
            pltpu.VMEM((2, 8, tile_cols), jnp.float32),
            pltpu.VMEM((2, 8, tile_rows), jnp.float32),
            pltpu.VMEM((4, 8, 128), jnp.float32),
            pltpu.VMEM((tile_rows + 16, tile_cols + 256), jnp.float32),
            pltpu.SemaphoreType.DMA((copies,)),
            pltpu.SemaphoreType.DMA((copies,)),
            pltpu.SemaphoreType.DMA((n - 1,)),
            pltpu.SemaphoreType.DMA((n - 1,)),
            pltpu.SemaphoreType.DMA((8,)),
            pltpu.SemaphoreType.DMA((8,)),
            pltpu.SemaphoreType.DMA((2,)),
        ],
        compiler_params=pltpu.CompilerParams(
            collective_id=0, has_side_effects=True, vmem_limit_bytes=VMEM_BYTES
        ),
        name="gather_tiles",
    )(heights, albedo, plan_by_dest)


def render_kernel(
    plans, pick, used, light, tile_ref, mats_ref, seen_ref, grads_ref, sums_ref, total, fields
):
    tile, slot = pl.program_id(0), pl.program_id(1)
    most = pl.num_programs(1)
    step = tile * most + slot
    size = seen_ref.shape[-1]

    @pl.when(slot == 0)
    def _():
        total[...] = jnp.zeros_like(total)
        _, tile_rows, tile_cols = fields.shape
        ahead = tile_rows + RIM_ROWS

        def real(first, count):
            return tile_ref[0, pl.ds(first, count)].astype(jnp.int32).astype(jnp.float32)

        heights = real(0, tile_rows)
        rim = real(tile_rows, RIM_ROWS)
        side = RIM_ROWS // 2
        gap = jnp.zeros((128 - RIM_ROWS, tile_cols), jnp.float32)
        sides = jnp.transpose(jnp.concatenate([rim[:side], gap, rim[side:]], axis=0))
        across = jnp.concatenate([heights, sides], axis=1)
        right = pltpu.roll(across, tile_cols + 127, 1)[:, :tile_cols]
        left = pltpu.roll(across, 1, 1)[:, :tile_cols]
        line = lax.broadcasted_iota(jnp.int32, (tile_rows, 1), 0)
        above = jnp.where(line == 0, rim[RIM_ROWS - 2 : RIM_ROWS - 1], pltpu.roll(heights, 1, 0))
        below = jnp.where(line == tile_rows - 1, rim[1:2], pltpu.roll(heights, tile_rows - 1, 0))
        up = real(ahead, tile_rows) * (1.0 / FIELD_SCALE)
        slope_up = up * (0.5 / HEIGHT_SCALE)
        fields[0] = (left - right) * slope_up
        fields[1] = (above - below) * slope_up
        fields[2] = up

    @pl.when(used[step] == 1)
    def _():
        image = pick[step]
        rows = pl.ds(pl.multiple_of(plans[tile, 0, slot], 128), size)
        cols = pl.ds(pl.multiple_of(plans[tile, 1, slot], 128), size)
        sun_x, sun_y, sun_z = light[0, image], light[1, image], light[2, image]
        gain = light[3, image]

        def field(k):
            return fields[k, rows, cols]

        shaded = (sun_x * field(0) + sun_y * field(1) + sun_z * field(2)).astype(jnp.bfloat16)
        first = jnp.dot(mats_ref[0, 0], shaded, preferred_element_type=jnp.float32)
        predicted = gain * lax.dot_general(
            first.astype(jnp.bfloat16),
            mats_ref[0, 1],
            (((1,), (1,)), ((), ())),
            preferred_element_type=jnp.float32,
        )
        residual = predicted - seen_ref[0].astype(jnp.float32)
        weighted = (gain * residual).astype(jnp.bfloat16)
        back = lax.dot_general(
            mats_ref[0, 0], weighted, (((0,), (0,)), ((), ())), preferred_element_type=jnp.float32
        ).astype(jnp.bfloat16)
        crop_grad = jnp.dot(back, mats_ref[0, 1], preferred_element_type=jnp.float32)

        col = lax.broadcasted_iota(jnp.int32, (1, size), 1)
        row = lax.broadcasted_iota(jnp.int32, (size, 1), 0)
        last = size - 1
        right = jnp.where(col == last, predicted, pltpu.roll(predicted, last, 1))
        left = jnp.where(col == 0, predicted, pltpu.roll(predicted, 1, 1))
        below = jnp.where(row == last, predicted, pltpu.roll(predicted, last, 0))
        above = jnp.where(row == 0, predicted, pltpu.roll(predicted, 1, 0))
        col_weight = jnp.where((col == 0) | (col == last), 1.0, 0.5)
        row_place = (row.astype(jnp.float32) - 0.5 * (size - 1)) / size
        by_u = residual * (right - left)
        by_v = residual * (below - above)
        ends = 0.5 * (by_v[0:1] + by_v[last:])
        tilt = 0.5 * (0.5 * (size - 1) / size) * (by_v[last:] - by_v[0:1])
        sums_ref[image, 0:1] = col_weight * jnp.sum(by_u, axis=0, keepdims=True)
        sums_ref[image, 1:2] = col_weight * jnp.sum(by_u * row_place, axis=0, keepdims=True)
        sums_ref[image, 2:3] = 0.5 * jnp.sum(by_v, axis=0, keepdims=True) + ends
        sums_ref[image, 3:4] = 0.5 * jnp.sum(by_v * row_place, axis=0, keepdims=True) + tilt
        sums_ref[image, 4:5] = jnp.sum(residual * predicted, axis=0, keepdims=True)
        sums_ref[image, 5:8] = jnp.zeros((3, size), jnp.float32)

        fx, fy, fz = field(0), field(1), field(2)
        along = (sun_x * fx + sun_y * fy + sun_z * fz) * pl.reciprocal(
            fx * fx + fy * fy + fz * fz, approx=True
        )
        scaled = crop_grad * fz
        total[0, rows, cols] += scaled * (fx * along - sun_x)
        total[1, rows, cols] += scaled * (fy * along - sun_y)

    @pl.when(slot == most - 1)
    def _():
        _, tile_rows, tile_cols = total.shape
        grad_x, grad_y = 0.5 * total[0], 0.5 * total[1]
        line = lax.broadcasted_iota(jnp.int32, (tile_rows, 1), 0)
        place = lax.broadcasted_iota(jnp.int32, (1, tile_cols), 1)
        left = jnp.where(place == 0, 0.0, pltpu.roll(grad_x, 1, 1))
        right = jnp.where(place == tile_cols - 1, 0.0, pltpu.roll(grad_x, tile_cols - 1, 1))
        above = jnp.where(line == 0, 0.0, pltpu.roll(grad_y, 1, 0))
        below = jnp.where(line == tile_rows - 1, 0.0, pltpu.roll(grad_y, tile_rows - 1, 0))
        spread = (left - right) + (above - below)
        grads_ref[0, 0:tile_rows] = spread.astype(grads_ref.dtype)
        at = lax.broadcasted_iota(jnp.int32, (RIM_ROWS, 1), 0)
        rim = jnp.where(at == 0, grad_y[0:1], 0.0)
        rim = jnp.where(at == 1, grad_y[tile_rows - 1 :], rim)
        rim = jnp.where(at == 2, columns_as_rows(grad_x, True)[0:1], rim)
        rim = jnp.where(at == 3, columns_as_rows(grad_x, False)[7:8], rim)
        grads_ref[0, pl.ds(tile_rows, RIM_ROWS)] = rim.astype(grads_ref.dtype)


def render(plans, pick, used, light, tiles, resample, observed, most):
    n, packed_rows, tile_cols = tiles.shape
    tile_rows = (packed_rows - RIM_ROWS) // 2
    crops, size, _ = observed.shape

    def crop_at(t, j, plans, pick, used):
        return pick[t * most + j]

    def inner(plans, pick, used, light, *refs):
        render_kernel(plans, pick, used, light, *refs)

    return pl.pallas_call(
        inner,
        out_shape=(
            jax.ShapeDtypeStruct((n, tile_rows + RIM_ROWS, tile_cols), jnp.bfloat16),
            jax.ShapeDtypeStruct((crops, 8, size), jnp.float32),
        ),
        grid_spec=pltpu.PrefetchScalarGridSpec(
            num_scalar_prefetch=3,
            grid=(n, most),
            in_specs=[
                pl.BlockSpec(memory_space=pltpu.SMEM),
                pl.BlockSpec((1, packed_rows, tile_cols), lambda t, j, *s: (t, 0, 0)),
                pl.BlockSpec((1, 2, size, size), lambda t, j, *s: (crop_at(t, j, *s), 0, 0, 0)),
                pl.BlockSpec((1, size, size), lambda t, j, *s: (crop_at(t, j, *s), 0, 0)),
            ],
            out_specs=(
                pl.BlockSpec((1, tile_rows + RIM_ROWS, tile_cols), lambda t, j, *s: (t, 0, 0)),
                pl.BlockSpec((crops, 8, size), lambda t, j, *s: (0, 0, 0)),
            ),
            scratch_shapes=[
                pltpu.VMEM((2, tile_rows, tile_cols), jnp.float32),
                pltpu.VMEM((3, tile_rows, tile_cols), jnp.float32),
            ],
        ),
        compiler_params=pltpu.CompilerParams(
            dimension_semantics=("arbitrary", "arbitrary"), vmem_limit_bytes=VMEM_BYTES
        ),
        name="render",
    )(plans, pick, used, light, tiles, resample, observed)


def scatter_kernel(
    n,
    n_dx,
    grads_ref,
    sums_ref,
    smooth_ref,
    height_ref,
    camera_ref,
    kept,
    first,
    later,
    out_ref,
    csums,
    rims,
    send,
    recv,
    csend,
    crecv,
    hsend,
    hrecv,
    lsem,
):
    bits = bit_count(n)
    me, across = lax.axis_index("dy"), lax.axis_index("dx")
    tile_rows, tile_cols = height_ref.shape
    half = tile_rows // 2
    greet(n, n_dx, False)

    number = iter(range(send.shape[0]))
    started = []

    def push(source, target, bit):
        c = next(number)
        copy = pltpu.make_async_remote_copy(
            src_ref=source,
            dst_ref=target,
            send_sem=send.at[c],
            recv_sem=recv.at[c],
            device_id={"dy": flipped(me, 1 << bit, bits)},
            device_id_type=MESH,
        )
        copy.start()
        started.append(copy)
        return copy

    masks = [m << 1 for m in range(n // 2)][::-1]
    pair = {}

    def push_pair(mask):
        pair[mask] = push(grads_ref.at[flipped(me, mask + 1, bits)], first.at[mask >> 1], 0)

    push_pair(masks[0])
    loads = {}
    for mask in masks:
        loads[mask] = pltpu.make_async_copy(
            grads_ref.at[flipped(me, mask, bits)], kept.at[mask >> 1], lsem.at[mask >> 1]
        )
        loads[mask].start()
    camera_copies = []
    for step in range(1, n):
        to = lax.rem(me + step, n)
        copy = pltpu.make_async_remote_copy(
            src_ref=sums_ref.at[to],
            dst_ref=csums.at[step - 1],
            send_sem=csend.at[step - 1],
            recv_sem=crecv.at[step - 1],
            device_id={"dy": to},
            device_id_type=MESH,
        )
        copy.start()
        camera_copies.append(copy)

    orders = bit_orders(bits)
    places = iter(range(later.shape[0]))
    coming = {}

    def rows(part):
        return pl.ds(part * half, half + part * RIM_ROWS)

    def landing(at, part):
        return later.at[at, pl.ds(0, half + part * RIM_ROWS), :]

    for mask in masks:
        loads[mask].wait()
        pair[mask].wait_recv()
        if mask:
            push_pair(mask - 2)
        mine = kept[mask >> 1].astype(jnp.float32)
        both = mine + first[mask >> 1].astype(jnp.float32)
        if mask == 0:
            out_ref[...] = both
        else:
            first[mask >> 1] = both.astype(first.dtype)
            for part, order in enumerate(orders):
                if mask >> order[0] & 1:
                    at = next(places)
                    source = first.at[mask >> 1, rows(part), :]
                    copy = push(source, landing(at, part), order[0])
                    coming[(part, mask ^ 1 << order[0])] = (copy, at)
    for stage in range(bits - 1):
        landed = sorted(coming.items(), key=lambda item: item[0][1] == 0)
        coming = {}
        for (part, mask), (copy, at) in landed:
            order = orders[part]
            copy.wait_recv()
            add = landing(at, part)[...].astype(jnp.float32)
            if mask == 0:
                out_ref[rows(part), :] += add
            else:
                held = first[mask >> 1, rows(part), :].astype(jnp.float32)
                first[mask >> 1, rows(part), :] = (held + add).astype(first.dtype)
                bit = order[stage + 1]
                if mask >> bit & 1:
                    to = next(places)
                    source = first.at[mask >> 1, rows(part), :]
                    sent = push(source, landing(to, part), bit)
                    coming[(part, mask ^ 1 << bit)] = (sent, to)
    targets = (
        {"dx": lax.rem(across + n_dx - 1, n_dx)},
        {"dx": lax.rem(across + 1, n_dx)},
        {"dy": lax.rem(me + n - 1, n)},
        {"dy": lax.rem(me + 1, n)},
    )
    halos = []
    for c, device in enumerate(targets):
        copy = pltpu.make_async_remote_copy(
            src_ref=out_ref.at[pl.ds(tile_rows, 8)],
            dst_ref=rims.at[c],
            send_sem=hsend.at[c],
            recv_sem=hrecv.at[c],
            device_id=device,
            device_id_type=MESH,
        )
        copy.start()
        halos.append(copy)
    camera = sums_ref[me]
    for step in range(1, n):
        camera_copies[step - 1].wait()
        camera = camera + csums[step - 1]
    camera_ref[...] = camera
    for copy in started:
        copy.wait_send()
    for copy in halos:
        copy.wait()

    after_x = jnp.where(across < n_dx - 1, rims[0], 0.0)
    before_x = jnp.where(across > 0, rims[1], 0.0)
    after_y = jnp.where(me < n - 1, rims[2], 0.0)[0:1]
    before_y = jnp.where(me > 0, rims[3], 0.0)[1:2]
    gap = jnp.zeros((112, tile_rows), jnp.float32)
    sides = jnp.transpose(jnp.concatenate([after_x, before_x, gap], axis=0))
    row = lax.broadcasted_iota(jnp.int32, (tile_rows, 1), 0)
    col = lax.broadcasted_iota(jnp.int32, (1, tile_cols), 1)
    rim = jnp.where(col == tile_cols - 1, -sides[:, 2:3], 0.0)
    rim = rim + jnp.where(col == 0, sides[:, 11:12], 0.0)
    rim = rim + jnp.where(row == tile_rows - 1, -after_y, 0.0)
    rim = rim + jnp.where(row == 0, before_y, 0.0)
    height_ref[...] = out_ref[0:tile_rows] + smooth_ref[...] + rim


def scatter_sums(grads, sums, smooth, n, n_dx):
    _, sent_rows, tile_cols = grads.shape
    tile_rows = smooth.shape[0]
    assert tile_rows == tile_cols
    high = n // 2
    halves = 2 * (high - 1)
    copies = high + halves
    vmem = pl.BlockSpec(memory_space=pltpu.VMEM)
    return pl.pallas_call(
        functools.partial(scatter_kernel, n, n_dx),
        out_shape=(
            jax.ShapeDtypeStruct(smooth.shape, jnp.float32),
            jax.ShapeDtypeStruct(sums.shape[1:], jnp.float32),
        ),
        in_specs=[pl.BlockSpec(memory_space=pl.ANY), vmem, vmem],
        out_specs=(vmem, vmem),
        scratch_shapes=[
            pltpu.VMEM((high, sent_rows, tile_cols), grads.dtype),
            pltpu.VMEM((high, sent_rows, tile_cols), grads.dtype),
            pltpu.VMEM((halves, sent_rows - tile_rows // 2, tile_cols), grads.dtype),
            pltpu.VMEM((sent_rows, tile_cols), jnp.float32),
            pltpu.VMEM((n - 1,) + sums.shape[1:], jnp.float32),
            pltpu.VMEM((4, 8, tile_cols), jnp.float32),
            pltpu.SemaphoreType.DMA((copies,)),
            pltpu.SemaphoreType.DMA((copies,)),
            pltpu.SemaphoreType.DMA((n - 1,)),
            pltpu.SemaphoreType.DMA((n - 1,)),
            pltpu.SemaphoreType.DMA((4,)),
            pltpu.SemaphoreType.DMA((4,)),
            pltpu.SemaphoreType.DMA((high,)),
        ],
        compiler_params=pltpu.CompilerParams(
            collective_id=1, has_side_effects=True, vmem_limit_bytes=VMEM_BYTES
        ),
        name="scatter_sums",
    )(grads, sums, smooth)


def per_device(
    heights, albedo, observed, resample, exposure, sun_azimuth, sun_elevation, send_plan, recv_plan
):
    n, n_dx = lax.axis_size("dy"), lax.axis_size("dx")
    crops, size = observed.shape[0], observed.shape[-1]
    slot_count = send_plan.shape[-1]
    most = slot_count // n
    receive = recv_plan[0, 0]
    sun_table = sun_vectors(sun_azimuth[0], sun_elevation[0])
    light = jnp.concatenate([sun_table, jnp.exp(exposure)])
    slot_ids = jnp.arange(slot_count, dtype=jnp.int32)
    reached = jnp.where(receive[None, :] <= slot_ids[:, None], receive[None, :], -1)
    pick = jnp.argmax(reached, axis=1).astype(jnp.int32)
    used = (jnp.max(reached, axis=1) == slot_ids).astype(jnp.int32)
    plan_by_dest = jnp.pad(
        send_plan[0, 0, 0:2].reshape(2, n, most).transpose(1, 0, 2),
        ((0, 0), (0, 6), (0, 128 - most)),
    )

    tiles, plans, smooth = gather_tiles(heights, albedo, plan_by_dest, n, n_dx)
    tile_grads, sums = render(plans, pick, used, light, tiles, resample, observed, most)
    height_gradient, camera = scatter_sums(
        tile_grads, sums.reshape(n, crops // n, 8, size), smooth, n, n_dx
    )

    coordinate = (jnp.arange(size, dtype=jnp.float32) - 0.5 * (size - 1)) / size
    plain = jnp.sum(camera, axis=-1)
    placed = jnp.sum(camera * coordinate, axis=-1)
    camera_model = jnp.stack(
        [
            plain[:, 0] / size,
            placed[:, 0] / size,
            plain[:, 1] / size,
            plain[:, 2] / size,
            placed[:, 2] / size,
            plain[:, 3] / size,
            plain[:, 4] / (size * size),
        ],
        axis=-1,
    )

    return (height_gradient, camera_model[None])


def solution(mesh):
    placed = (
        P("dy", "dx"),
        P("dy", "dx"),
        P(("dy", "dx"), None, None),
        P(("dy", "dx"), None, None, None),
        P("dx", None),
        P("dx", None),
        P("dx", None),
        P("dy", "dx", None, None),
        P("dy", "dx", None),
    )
    return jax.shard_map(
        per_device,
        mesh=mesh,
        in_specs=placed,
        out_specs=(P("dy", "dx"), P("dx", "dy", None)),
        check_vma=False,
    )
```

```python
import functools

import jax
import jax.numpy as jnp
from jax import lax
from jax.experimental import pallas as pl
from jax.experimental.pallas import tpu as pltpu
from jax.sharding import PartitionSpec as P

SMOOTHING_WEIGHT = 0.02
MESH = pl.DeviceIdType.MESH
VMEM_BYTES = 56 * 1024 * 1024
HEIGHT_SCALE = 8191.0
FIELD_SCALE = 21844.0
RIM_ROWS = 16


def fixed_point(values, scale):
    return jnp.floor(values * scale + 0.5).astype(jnp.int32).astype(jnp.int16)


def sun_vectors(solar_azimuth, elevation):
    return jnp.stack(
        [
            jnp.cos(elevation) * jnp.cos(solar_azimuth),
            jnp.cos(elevation) * jnp.sin(solar_azimuth),
            jnp.sin(elevation),
        ]
    )


def bit_count(count):
    bits = count.bit_length() - 1
    assert 1 << bits == count
    return bits


def flipped(index, mask, bits):
    for bit in range(bits):
        if mask >> bit & 1:
            weight = 1 << bit
            index = index + weight * (1 - 2 * ((index // weight) % 2))
    return index


def bit_orders(bits):
    up = list(range(1, bits))
    return (up, up[::-1])


def all_masks(order):
    masks = [0]
    for bit in order:
        masks = masks + [mask | 1 << bit for mask in masks]
    return masks


def columns_as_rows(block, low):
    width = block.shape[1]
    if low:
        return jnp.transpose(block[:, :128])[:8]
    return jnp.transpose(block[:, width - 128 :])[120:]


def rows_as_columns(rows, low):
    empty = jnp.zeros((120, rows.shape[1]), rows.dtype)
    parts = [empty, rows] if low else [rows, empty]
    return jnp.transpose(jnp.concatenate(parts, axis=0))


def greet(n, n_dx, corners):
    me, across = lax.axis_index("dy"), lax.axis_index("dx")
    barrier = pltpu.get_barrier_semaphore()
    for step in range(1, n):
        pl.semaphore_signal(
            barrier, inc=1, device_id={"dy": lax.rem(me + step, n)}, device_id_type=MESH
        )
    for side in (1, n_dx - 1):
        for up in (0, 1, n - 1) if corners else (0,):
            pl.semaphore_signal(
                barrier,
                inc=1,
                device_id={"dy": lax.rem(me + up, n), "dx": lax.rem(across + side, n_dx)},
                device_id_type=MESH,
            )
    pl.semaphore_wait(barrier, n - 1 + (6 if corners else 2))


def gather_kernel(
    n,
    n_dx,
    copies,
    heights_ref,
    albedo_ref,
    plan_ref,
    out_ref,
    plans_ref,
    smooth_ref,
    own_ref,
    edges,
    row_rim,
    col_rim,
    corner_rim,
    wide,
    send,
    recv,
    psend,
    precv,
    hsend,
    hrecv,
    lsem,
):
    bits = bit_count(n)
    me, across = lax.axis_index("dy"), lax.axis_index("dx")
    tile_rows, tile_cols = heights_ref.shape
    cut = tile_rows + RIM_ROWS
    heights = heights_ref[...]
    own_ref[0:tile_rows] = fixed_point(heights, HEIGHT_SCALE)
    edges[0] = columns_as_rows(heights, True)
    edges[1] = columns_as_rows(heights, False)
    greet(n, n_dx, True)

    row_parts = (pl.ds(0, 8), pl.ds(tile_rows - 8, 8))
    col_parts = (pl.ds(0, 128), pl.ds(tile_cols - 128, 128))
    row_to = (lax.rem(me + n - 1, n), lax.rem(me + 1, n))
    col_to = (lax.rem(across + n_dx - 1, n_dx), lax.rem(across + 1, n_dx))
    halos = []

    def halo(source, target, device):
        c = len(halos)
        copy = pltpu.make_async_remote_copy(
            src_ref=source,
            dst_ref=target,
            send_sem=hsend.at[c],
            recv_sem=hrecv.at[c],
            device_id=device,
            device_id_type=MESH,
        )
        copy.start()
        halos.append(copy)

    for up in range(2):
        halo(edges.at[up], col_rim.at[up], {"dx": col_to[up]})
    for up in range(2):
        halo(heights_ref.at[row_parts[up]], row_rim.at[up], {"dy": row_to[up]})
    for up in range(2):
        for right in range(2):
            halo(
                heights_ref.at[row_parts[up], col_parts[right]],
                corner_rim.at[up * 2 + right],
                {"dy": row_to[up], "dx": col_to[right]},
            )
    number = iter(range(copies))

    def rows(part):
        return pl.ds(part * tile_rows, cut if part else tile_rows)

    def make(mask, part, bit):
        tile = flipped(me, mask, bits)
        source = own_ref if mask == 0 else out_ref.at[tile]
        c = next(number)
        return pltpu.make_async_remote_copy(
            src_ref=source.at[rows(part), :],
            dst_ref=out_ref.at[tile, rows(part), :],
            send_sem=send.at[c],
            recv_sem=recv.at[c],
            device_id={"dy": flipped(me, 1 << bit, bits)},
            device_id_type=MESH,
        )

    orders = bit_orders(bits)
    started = []
    arriving = {}

    def forward(mask, part, over):
        copy = make(mask, part, over)
        copy.start()
        started.append(copy)
        arriving[(mask | 1 << over, part)] = copy

    def later(mask, order):
        seen = [k for k, bit in enumerate(order) if mask >> bit & 1]
        return order[(max(seen) + 1 if seen else 0) :]

    for position in range(bits - 1):
        forward(0, 0, orders[0][position])
    for copy in halos:
        copy.wait_recv()

    top, bottom = row_rim[1], row_rim[0]
    wide[...] = jnp.zeros_like(wide)
    inner_rows, inner_cols = pl.ds(8, tile_rows), pl.ds(128, tile_cols)
    wide[inner_rows, inner_cols] = heights
    wide[0:8, inner_cols] = jnp.where(me > 0, top, 0.0)
    wide[pl.ds(8 + tile_rows, 8), inner_cols] = jnp.where(me < n - 1, bottom, 0.0)
    wide[inner_rows, 0:128] = jnp.where(across > 0, rows_as_columns(col_rim[1], True), 0.0)
    wide[inner_rows, pl.ds(128 + tile_cols, 128)] = jnp.where(
        across < n_dx - 1, rows_as_columns(col_rim[0], False), 0.0
    )
    for up in range(2):
        for right in range(2):
            inside = (me > 0 if up else me < n - 1) & (across > 0 if right else across < n_dx - 1)
            wide[
                pl.ds(0 if up else 8 + tile_rows, 8), pl.ds(0 if right else 128 + tile_cols, 128)
            ] = jnp.where(inside, corner_rim[up * 2 + right], 0.0)

    def inner(block):
        return block[8 : 8 + tile_rows, 128 : 128 + tile_cols]

    def around(block):
        rows_all, cols_all = block.shape
        return (
            pltpu.roll(block, 1, 0),
            pltpu.roll(block, rows_all - 1, 0),
            pltpu.roll(block, 1, 1),
            pltpu.roll(block, cols_all - 1, 1),
        )

    place = lax.broadcasted_iota(jnp.int32, (RIM_ROWS, 1), 0)
    rim = jnp.where(place == 0, jnp.where(across < n_dx - 1, col_rim[0], 0.0)[0:1], 0.0)
    rim = jnp.where(place == 1, jnp.where(me < n - 1, row_rim[0], 0.0)[0:1], rim)
    rim = jnp.where(place == RIM_ROWS - 2, jnp.where(me > 0, row_rim[1], 0.0)[7:8], rim)
    rim = jnp.where(place == RIM_ROWS - 1, jnp.where(across > 0, col_rim[1], 0.0)[7:8], rim)
    own_ref[pl.ds(tile_rows, RIM_ROWS)] = fixed_point(rim, HEIGHT_SCALE)

    above, below, left, right = around(wide[...])
    slope_x = inner(right - left) * 0.5
    slope_y = inner(below - above) * 0.5
    up = albedo_ref[...] * lax.rsqrt(1.0 + slope_x * slope_x + slope_y * slope_y)
    own_ref[pl.ds(cut, tile_rows)] = fixed_point(up, FIELD_SCALE)
    for position in range(bits - 1):
        forward(0, 1, orders[1][position])
    plan_copies = []
    for step in range(1, n):
        to = lax.rem(me + step, n)
        copy = pltpu.make_async_remote_copy(
            src_ref=plan_ref.at[to],
            dst_ref=plans_ref.at[me],
            send_sem=psend.at[step - 1],
            recv_sem=precv.at[step - 1],
            device_id={"dy": to},
            device_id_type=MESH,
        )
        copy.start()
        plan_copies.append(copy)
    for part in range(2):
        forward(0, part, 0)
    local = pltpu.make_async_copy(own_ref, out_ref.at[me], lsem.at[0])
    local.start()
    local_plan = pltpu.make_async_copy(plan_ref.at[me], plans_ref.at[me], lsem.at[1])
    local_plan.start()

    center = wide[...]
    above, below, left, right = around(center)
    lap = above + below + left + right - 4.0 * center
    row = lax.broadcasted_iota(jnp.int32, (center.shape[0], 1), 0)
    col = lax.broadcasted_iota(jnp.int32, (1, center.shape[1]), 1)
    row_keep = ((row >= 8) | (me > 0)) & ((row < 8 + tile_rows) | (me < n - 1))
    col_keep = ((col >= 128) | (across > 0)) & ((col < 128 + tile_cols) | (across < n_dx - 1))
    lap = jnp.where(row_keep & col_keep, lap, 0.0)
    above, below, left, right = around(lap)
    smooth_ref[...] = SMOOTHING_WEIGHT * inner(above + below + left + right - 4.0 * lap)

    mask_lists = [all_masks(order)[1:] for order in orders]
    for position in range(len(mask_lists[0])):
        for part, order in enumerate(orders):
            mask = mask_lists[part][position]
            arriving[(mask, part)].wait_recv()
            for bit in later(mask, order):
                forward(mask, part, bit)
            forward(mask, part, 0)
    for (mask, part), copy in arriving.items():
        if mask & 1:
            copy.wait_recv()
    for copy in started:
        copy.wait_send()
    for copy in plan_copies:
        copy.wait()
    for copy in halos:
        copy.wait_send()
    local.wait()
    local_plan.wait()


def gather_tiles(heights, albedo, plan_by_dest, n, n_dx):
    copies = 2 * (n // 2 - 1) + n
    tile_rows, tile_cols = heights.shape
    vmem = pl.BlockSpec(memory_space=pltpu.VMEM)
    hbm = pl.BlockSpec(memory_space=pl.ANY)
    return pl.pallas_call(
        functools.partial(gather_kernel, n, n_dx, copies),
        out_shape=(
            jax.ShapeDtypeStruct((n, 2 * tile_rows + RIM_ROWS, tile_cols), jnp.int16),
            jax.ShapeDtypeStruct(plan_by_dest.shape, plan_by_dest.dtype),
            jax.ShapeDtypeStruct(heights.shape, jnp.float32),
        ),
        in_specs=[vmem, vmem, hbm],
        out_specs=(hbm, hbm, vmem),
        scratch_shapes=[
            pltpu.VMEM((2 * tile_rows + RIM_ROWS, tile_cols), jnp.int16),
            pltpu.VMEM((2, 8, tile_rows), jnp.float32),
            pltpu.VMEM((2, 8, tile_cols), jnp.float32),
            pltpu.VMEM((2, 8, tile_rows), jnp.float32),
            pltpu.VMEM((4, 8, 128), jnp.float32),
            pltpu.VMEM((tile_rows + 16, tile_cols + 256), jnp.float32),
            pltpu.SemaphoreType.DMA((copies,)),
            pltpu.SemaphoreType.DMA((copies,)),
            pltpu.SemaphoreType.DMA((n - 1,)),
            pltpu.SemaphoreType.DMA((n - 1,)),
            pltpu.SemaphoreType.DMA((8,)),
            pltpu.SemaphoreType.DMA((8,)),
            pltpu.SemaphoreType.DMA((2,)),
        ],
        compiler_params=pltpu.CompilerParams(
            collective_id=0, has_side_effects=True, vmem_limit_bytes=VMEM_BYTES
        ),
        name="gather_tiles",
    )(heights, albedo, plan_by_dest)


def render_kernel(
    plans, pick, light, tile_ref, mats_ref, seen_ref, grads_ref, sums_ref, total, fields
):
    tile, slot = pl.program_id(0), pl.program_id(1)
    most = pl.num_programs(1)
    step = tile * most + slot
    size = seen_ref.shape[-1]

    @pl.when(slot == 0)
    def _():
        total[...] = jnp.zeros_like(total)
        _, tile_rows, tile_cols = fields.shape
        ahead = tile_rows + RIM_ROWS

        def real(first, count):
            return tile_ref[0, pl.ds(first, count)].astype(jnp.int32).astype(jnp.float32)

        heights = real(0, tile_rows)
        rim = real(tile_rows, RIM_ROWS)
        side = RIM_ROWS // 2
        gap = jnp.zeros((128 - RIM_ROWS, tile_cols), jnp.float32)
        sides = jnp.transpose(jnp.concatenate([rim[:side], gap, rim[side:]], axis=0))
        across = jnp.concatenate([heights, sides], axis=1)
        right = pltpu.roll(across, tile_cols + 127, 1)[:, :tile_cols]
        left = pltpu.roll(across, 1, 1)[:, :tile_cols]
        line = lax.broadcasted_iota(jnp.int32, (tile_rows, 1), 0)
        above = jnp.where(line == 0, rim[RIM_ROWS - 2 : RIM_ROWS - 1], pltpu.roll(heights, 1, 0))
        below = jnp.where(line == tile_rows - 1, rim[1:2], pltpu.roll(heights, tile_rows - 1, 0))
        up = real(ahead, tile_rows) * (1.0 / FIELD_SCALE)
        slope_up = up * (0.5 / HEIGHT_SCALE)
        fields[0] = (left - right) * slope_up
        fields[1] = (above - below) * slope_up
        fields[2] = up

    crops = sums_ref.shape[0]

    @pl.when(pick[step] >= crops)
    def _():
        image = pick[step] - crops
        rows = pl.ds(pl.multiple_of(plans[tile, 0, slot], 128), size)
        cols = pl.ds(pl.multiple_of(plans[tile, 1, slot], 128), size)
        sun_x, sun_y, sun_z = light[0, image], light[1, image], light[2, image]
        gain = light[3, image]

        def field(k):
            return fields[k, rows, cols]

        shaded = (sun_x * field(0) + sun_y * field(1) + sun_z * field(2)).astype(jnp.bfloat16)
        first = jnp.dot(mats_ref[0, 0], shaded, preferred_element_type=jnp.float32)
        predicted = gain * lax.dot_general(
            first.astype(jnp.bfloat16),
            mats_ref[0, 1],
            (((1,), (1,)), ((), ())),
            preferred_element_type=jnp.float32,
        )
        residual = predicted - seen_ref[0].astype(jnp.float32)
        weighted = (gain * residual).astype(jnp.bfloat16)
        back = lax.dot_general(
            mats_ref[0, 0], weighted, (((0,), (0,)), ((), ())), preferred_element_type=jnp.float32
        ).astype(jnp.bfloat16)
        crop_grad = jnp.dot(back, mats_ref[0, 1], preferred_element_type=jnp.float32)

        col = lax.broadcasted_iota(jnp.int32, (1, size), 1)
        row = lax.broadcasted_iota(jnp.int32, (size, 1), 0)
        last = size - 1
        right = jnp.where(col == last, predicted, pltpu.roll(predicted, last, 1))
        left = jnp.where(col == 0, predicted, pltpu.roll(predicted, 1, 1))
        below = jnp.where(row == last, predicted, pltpu.roll(predicted, last, 0))
        above = jnp.where(row == 0, predicted, pltpu.roll(predicted, 1, 0))
        col_weight = jnp.where((col == 0) | (col == last), 1.0, 0.5)
        row_place = (row.astype(jnp.float32) - 0.5 * (size - 1)) / size
        by_u = residual * (right - left)
        by_v = residual * (below - above)
        ends = 0.5 * (by_v[0:1] + by_v[last:])
        tilt = 0.5 * (0.5 * (size - 1) / size) * (by_v[last:] - by_v[0:1])
        sums_ref[image, 0:1] = col_weight * jnp.sum(by_u, axis=0, keepdims=True)
        sums_ref[image, 1:2] = col_weight * jnp.sum(by_u * row_place, axis=0, keepdims=True)
        sums_ref[image, 2:3] = 0.5 * jnp.sum(by_v, axis=0, keepdims=True) + ends
        sums_ref[image, 3:4] = 0.5 * jnp.sum(by_v * row_place, axis=0, keepdims=True) + tilt
        sums_ref[image, 4:5] = jnp.sum(residual * predicted, axis=0, keepdims=True)
        sums_ref[image, 5:8] = jnp.zeros((3, size), jnp.float32)

        fx, fy, fz = field(0), field(1), field(2)
        along = (sun_x * fx + sun_y * fy + sun_z * fz) * pl.reciprocal(
            fx * fx + fy * fy + fz * fz, approx=True
        )
        scaled = crop_grad * fz
        total[0, rows, cols] += scaled * (fx * along - sun_x)
        total[1, rows, cols] += scaled * (fy * along - sun_y)

    @pl.when(slot == most - 1)
    def _():
        _, tile_rows, tile_cols = total.shape
        grad_x, grad_y = 0.5 * total[0], 0.5 * total[1]
        line = lax.broadcasted_iota(jnp.int32, (tile_rows, 1), 0)
        place = lax.broadcasted_iota(jnp.int32, (1, tile_cols), 1)
        left = jnp.where(place == 0, 0.0, pltpu.roll(grad_x, 1, 1))
        right = jnp.where(place == tile_cols - 1, 0.0, pltpu.roll(grad_x, tile_cols - 1, 1))
        above = jnp.where(line == 0, 0.0, pltpu.roll(grad_y, 1, 0))
        below = jnp.where(line == tile_rows - 1, 0.0, pltpu.roll(grad_y, tile_rows - 1, 0))
        spread = (left - right) + (above - below)
        grads_ref[0, 0:tile_rows] = spread.astype(grads_ref.dtype)
        at = lax.broadcasted_iota(jnp.int32, (RIM_ROWS, 1), 0)
        rim = jnp.where(at == 0, grad_y[0:1], 0.0)
        rim = jnp.where(at == 1, grad_y[tile_rows - 1 :], rim)
        rim = jnp.where(at == 2, columns_as_rows(grad_x, True)[0:1], rim)
        rim = jnp.where(at == 3, columns_as_rows(grad_x, False)[7:8], rim)
        grads_ref[0, pl.ds(tile_rows, RIM_ROWS)] = rim.astype(grads_ref.dtype)


def render(plans, pick, light, tiles, resample, observed, most):
    n, packed_rows, tile_cols = tiles.shape
    tile_rows = (packed_rows - RIM_ROWS) // 2
    crops, size, _ = observed.shape

    def crop_at(t, j, plans, pick):
        return pick[t * most + j] % crops

    return pl.pallas_call(
        render_kernel,
        out_shape=(
            jax.ShapeDtypeStruct((n, tile_rows + RIM_ROWS, tile_cols), jnp.bfloat16),
            jax.ShapeDtypeStruct((crops, 8, size), jnp.float32),
        ),
        grid_spec=pltpu.PrefetchScalarGridSpec(
            num_scalar_prefetch=2,
            grid=(n, most),
            in_specs=[
                pl.BlockSpec(memory_space=pltpu.SMEM),
                pl.BlockSpec((1, packed_rows, tile_cols), lambda t, j, *s: (t, 0, 0)),
                pl.BlockSpec((1, 2, size, size), lambda t, j, *s: (crop_at(t, j, *s), 0, 0, 0)),
                pl.BlockSpec((1, size, size), lambda t, j, *s: (crop_at(t, j, *s), 0, 0)),
            ],
            out_specs=(
                pl.BlockSpec((1, tile_rows + RIM_ROWS, tile_cols), lambda t, j, *s: (t, 0, 0)),
                pl.BlockSpec((crops, 8, size), lambda t, j, *s: (0, 0, 0)),
            ),
            scratch_shapes=[
                pltpu.VMEM((2, tile_rows, tile_cols), jnp.float32),
                pltpu.VMEM((3, tile_rows, tile_cols), jnp.float32),
            ],
        ),
        compiler_params=pltpu.CompilerParams(
            dimension_semantics=("arbitrary", "arbitrary"), vmem_limit_bytes=VMEM_BYTES
        ),
        name="render",
    )(plans, pick, light, tiles, resample, observed)


def scatter_kernel(
    n,
    n_dx,
    grads_ref,
    sums_ref,
    smooth_ref,
    height_ref,
    camera_ref,
    kept,
    first,
    later,
    out_ref,
    csums,
    rims,
    send,
    recv,
    csend,
    crecv,
    hsend,
    hrecv,
    lsem,
):
    bits = bit_count(n)
    me, across = lax.axis_index("dy"), lax.axis_index("dx")
    tile_rows, tile_cols = height_ref.shape
    half = tile_rows // 2
    greet(n, n_dx, False)

    number = iter(range(send.shape[0]))
    started = []

    def push(source, target, bit):
        c = next(number)
        copy = pltpu.make_async_remote_copy(
            src_ref=source,
            dst_ref=target,
            send_sem=send.at[c],
            recv_sem=recv.at[c],
            device_id={"dy": flipped(me, 1 << bit, bits)},
            device_id_type=MESH,
        )
        copy.start()
        started.append(copy)
        return copy

    masks = [m << 1 for m in range(n // 2)][::-1]
    pair = {}

    def push_pair(mask):
        pair[mask] = push(grads_ref.at[flipped(me, mask + 1, bits)], first.at[mask >> 1], 0)

    push_pair(masks[0])
    loads = {}
    for mask in masks:
        loads[mask] = pltpu.make_async_copy(
            grads_ref.at[flipped(me, mask, bits)], kept.at[mask >> 1], lsem.at[mask >> 1]
        )
        loads[mask].start()
    camera_copies = []
    for step in range(1, n):
        to = lax.rem(me + step, n)
        copy = pltpu.make_async_remote_copy(
            src_ref=sums_ref.at[to],
            dst_ref=csums.at[step - 1],
            send_sem=csend.at[step - 1],
            recv_sem=crecv.at[step - 1],
            device_id={"dy": to},
            device_id_type=MESH,
        )
        copy.start()
        camera_copies.append(copy)

    orders = bit_orders(bits)
    places = iter(range(later.shape[0]))
    coming = {}

    def rows(part):
        return pl.ds(part * half, half + part * RIM_ROWS)

    def landing(at, part):
        return later.at[at, pl.ds(0, half + part * RIM_ROWS), :]

    for mask in masks:
        loads[mask].wait()
        pair[mask].wait_recv()
        if mask:
            push_pair(mask - 2)
        mine = kept[mask >> 1].astype(jnp.float32)
        both = mine + first[mask >> 1].astype(jnp.float32)
        if mask == 0:
            out_ref[...] = both
        else:
            first[mask >> 1] = both.astype(first.dtype)
            for part, order in enumerate(orders):
                if mask >> order[0] & 1:
                    at = next(places)
                    source = first.at[mask >> 1, rows(part), :]
                    copy = push(source, landing(at, part), order[0])
                    coming[(part, mask ^ 1 << order[0])] = (copy, at)
    for stage in range(bits - 1):
        landed = sorted(coming.items(), key=lambda item: item[0][1] == 0)
        coming = {}
        for (part, mask), (copy, at) in landed:
            order = orders[part]
            copy.wait_recv()
            add = landing(at, part)[...].astype(jnp.float32)
            if mask == 0:
                out_ref[rows(part), :] += add
            else:
                held = first[mask >> 1, rows(part), :].astype(jnp.float32)
                first[mask >> 1, rows(part), :] = (held + add).astype(first.dtype)
                bit = order[stage + 1]
                if mask >> bit & 1:
                    to = next(places)
                    source = first.at[mask >> 1, rows(part), :]
                    sent = push(source, landing(to, part), bit)
                    coming[(part, mask ^ 1 << bit)] = (sent, to)
    targets = (
        {"dx": lax.rem(across + n_dx - 1, n_dx)},
        {"dx": lax.rem(across + 1, n_dx)},
        {"dy": lax.rem(me + n - 1, n)},
        {"dy": lax.rem(me + 1, n)},
    )
    halos = []
    for c, device in enumerate(targets):
        copy = pltpu.make_async_remote_copy(
            src_ref=out_ref.at[pl.ds(tile_rows, 8)],
            dst_ref=rims.at[c],
            send_sem=hsend.at[c],
            recv_sem=hrecv.at[c],
            device_id=device,
            device_id_type=MESH,
        )
        copy.start()
        halos.append(copy)
    camera = sums_ref[me]
    for step in range(1, n):
        camera_copies[step - 1].wait()
        camera = camera + csums[step - 1]
    camera_ref[...] = camera
    for copy in started:
        copy.wait_send()
    for copy in halos:
        copy.wait()

    after_x = jnp.where(across < n_dx - 1, rims[0], 0.0)
    before_x = jnp.where(across > 0, rims[1], 0.0)
    after_y = jnp.where(me < n - 1, rims[2], 0.0)[0:1]
    before_y = jnp.where(me > 0, rims[3], 0.0)[1:2]
    gap = jnp.zeros((112, tile_rows), jnp.float32)
    sides = jnp.transpose(jnp.concatenate([after_x, before_x, gap], axis=0))
    row = lax.broadcasted_iota(jnp.int32, (tile_rows, 1), 0)
    col = lax.broadcasted_iota(jnp.int32, (1, tile_cols), 1)
    rim = jnp.where(col == tile_cols - 1, -sides[:, 2:3], 0.0)
    rim = rim + jnp.where(col == 0, sides[:, 11:12], 0.0)
    rim = rim + jnp.where(row == tile_rows - 1, -after_y, 0.0)
    rim = rim + jnp.where(row == 0, before_y, 0.0)
    height_ref[...] = out_ref[0:tile_rows] + smooth_ref[...] + rim


def scatter_sums(grads, sums, smooth, n, n_dx):
    _, sent_rows, tile_cols = grads.shape
    tile_rows = smooth.shape[0]
    assert tile_rows == tile_cols
    high = n // 2
    halves = 2 * (high - 1)
    copies = high + halves
    vmem = pl.BlockSpec(memory_space=pltpu.VMEM)
    return pl.pallas_call(
        functools.partial(scatter_kernel, n, n_dx),
        out_shape=(
            jax.ShapeDtypeStruct(smooth.shape, jnp.float32),
            jax.ShapeDtypeStruct(sums.shape[1:], jnp.float32),
        ),
        in_specs=[pl.BlockSpec(memory_space=pl.ANY), vmem, vmem],
        out_specs=(vmem, vmem),
        scratch_shapes=[
            pltpu.VMEM((high, sent_rows, tile_cols), grads.dtype),
            pltpu.VMEM((high, sent_rows, tile_cols), grads.dtype),
            pltpu.VMEM((halves, sent_rows - tile_rows // 2, tile_cols), grads.dtype),
            pltpu.VMEM((sent_rows, tile_cols), jnp.float32),
            pltpu.VMEM((n - 1,) + sums.shape[1:], jnp.float32),
            pltpu.VMEM((4, 8, tile_cols), jnp.float32),
            pltpu.SemaphoreType.DMA((copies,)),
            pltpu.SemaphoreType.DMA((copies,)),
            pltpu.SemaphoreType.DMA((n - 1,)),
            pltpu.SemaphoreType.DMA((n - 1,)),
            pltpu.SemaphoreType.DMA((4,)),
            pltpu.SemaphoreType.DMA((4,)),
            pltpu.SemaphoreType.DMA((high,)),
        ],
        compiler_params=pltpu.CompilerParams(
            collective_id=1, has_side_effects=True, vmem_limit_bytes=VMEM_BYTES
        ),
        name="scatter_sums",
    )(grads, sums, smooth)


def per_device(
    heights, albedo, observed, resample, exposure, sun_azimuth, sun_elevation, send_plan, recv_plan
):
    n, n_dx = lax.axis_size("dy"), lax.axis_size("dx")
    crops, size = observed.shape[0], observed.shape[-1]
    slot_count = send_plan.shape[-1]
    most = slot_count // n
    receive = recv_plan[0, 0]
    sun_table = sun_vectors(sun_azimuth[0], sun_elevation[0])
    light = jnp.concatenate([sun_table, jnp.exp(exposure)])
    slot_ids = jnp.arange(slot_count, dtype=jnp.int32)
    keys = receive * crops + jnp.arange(crops, dtype=jnp.int32)
    latest = jnp.max(jnp.where(receive[None, :] <= slot_ids[:, None], keys[None, :], 0), axis=1)
    filled = jnp.where(jnp.any(receive[None, :] == slot_ids[:, None], axis=1), crops, 0)
    pick = latest % crops + filled
    plan_by_dest = jnp.pad(
        send_plan[0, 0, 0:2].reshape(2, n, most).transpose(1, 0, 2),
        ((0, 0), (0, 6), (0, 128 - most)),
    )

    tiles, plans, smooth = gather_tiles(heights, albedo, plan_by_dest, n, n_dx)
    tile_grads, sums = render(plans, pick, light, tiles, resample, observed, most)
    height_gradient, camera = scatter_sums(
        tile_grads, sums.reshape(n, crops // n, 8, size), smooth, n, n_dx
    )

    coordinate = (jnp.arange(size, dtype=jnp.float32) - 0.5 * (size - 1)) / size
    plain = jnp.sum(camera, axis=-1)
    placed = jnp.sum(camera * coordinate, axis=-1)
    camera_model = jnp.stack(
        [
            plain[:, 0] / size,
            placed[:, 0] / size,
            plain[:, 1] / size,
            plain[:, 2] / size,
            placed[:, 2] / size,
            plain[:, 3] / size,
            plain[:, 4] / (size * size),
        ],
        axis=-1,
    )

    return (height_gradient, camera_model[None])


def solution(mesh):
    placed = (
        P("dy", "dx"),
        P("dy", "dx"),
        P(("dy", "dx"), None, None),
        P(("dy", "dx"), None, None, None),
        P("dx", None),
        P("dx", None),
        P("dx", None),
        P("dy", "dx", None, None),
        P("dy", "dx", None),
    )
    return jax.shard_map(
        per_device,
        mesh=mesh,
        in_specs=placed,
        out_specs=(P("dy", "dx"), P("dx", "dy", None)),
        check_vma=False,
    )
```
